256 devices in a mesh: ctx: 64 (over z, y_hi, x), tp: 4 (over y_lo, core).
Axes of the slice: x: 4, y: 4 (y_hi: 2, y_lo: 2; y = y_hi * 2 + y_lo), z: 8, core: 2. Of those that a mesh axis runs over, the one named last changes fastest.
Arguments:
- queries: bfloat16 [8192, 8192], P(('ctx', 'tp')), may hold values from -200 to 200
- key_head_states: bfloat16 [8192, 1024], P(('ctx', 'tp')), may hold values from -6 to 6
- value_head_states: bfloat16 [8192, 1024], P(('ctx', 'tp')), may hold values from -6 to 6
- output_gradient: bfloat16 [8192, 8192], P(('ctx', 'tp')), may hold values from -6 to 6
- doc_starts: int32 [16], replicated, may hold values from 0 to 8191, as said below
- span_map: int32 [128], replicated, may hold values from 0 to 127, as said below
Outputs:
- query_grad: bfloat16 [8192, 8192], P(('ctx', 'tp'))
- key_grad: bfloat16 [8192, 1024], P(('ctx', 'tp'))
- value_grad: bfloat16 [8192, 1024], P(('ctx', 'tp'))
The draws below stay inside these ranges and needn't reach their ends.
Inputs may be any that keep to these rules, and one draw needn't show every extreme that they name: `span_map`: entries 2c and 2c + 1 are the spans held in row block c of 128 rows: a mirrored pair m and 127 - m with m < 64. Every span appears once. `doc_starts`: strictly increasing, the first is 0. The sequence is four stretches of 2048 positions that no document crosses; one stretch is a single document, each other stretch holds five.
All inputs are finite; a program needn't handle non-finite values.
Results may differ from the reference program's by a relative error of at most 0.0075.
Values may be sent and summed in bfloat16 or wider, within the bound.
A program may use at most 128 MiB of HBM per device.

```python
import jax
import jax.numpy as jnp
from jax import lax

QUERY_HEADS = 64
KEY_VALUE_HEADS = 8
HEAD_WIDTH = 128
TOK_DEV = 128
DOCS = 16
SPAN = 64
SEQUENCE_TOKENS = 8192


def layout(key):
    map_key = jax.random.fold_in(key, 101)
    doc_key = jax.random.fold_in(key, 202)
    pair_count = SEQUENCE_TOKENS // TOK_DEV
    pair_order = jax.random.permutation(map_key, pair_count).astype(jnp.int32)
    span_table = jnp.stack([pair_order, 2 * pair_count - 1 - pair_order], axis=1).reshape(-1)
    stretch = SEQUENCE_TOKENS // 4
    single = jax.random.randint(jax.random.fold_in(doc_key, 7), (), 0, 4)
    candidates = []
    for region in range(4):
        cut_key = jax.random.fold_in(doc_key, region)
        cut_points = jnp.sort(jax.random.permutation(cut_key, stretch - 1)[:4] + 1).astype(jnp.int32)
        cut_points = jnp.where(single == region, SEQUENCE_TOKENS + cut_points, region * stretch + cut_points)
        candidates.append(jnp.concatenate([jnp.full((1,), region * stretch, jnp.int32), cut_points]))
    starts = jnp.sort(jnp.concatenate(candidates))[:DOCS].astype(jnp.int32)
    return (span_table, starts)


def fields(key, align_part):
    span_table, starts = layout(key)
    random_seed_key = jax.random.fold_in(key, 303)
    row_ids = jnp.arange(SEQUENCE_TOKENS, dtype=jnp.int32)
    positions = span_table[row_ids // SPAN] * SPAN + row_ids % SPAN
    covered = jnp.sum((positions[:, None] >= starts[None, :]).astype(jnp.int32), axis=1)
    earlier = jnp.roll(covered, 1)
    chosen = (row_ids % 16 == 7) & (covered == earlier) & (align_part > 0.5)
    levels = jax.random.uniform(jax.random.fold_in(random_seed_key, 4), (SEQUENCE_TOKENS,), jnp.float32, 9.0, 25.0)
    gaussian_keys = jnp.clip(jax.random.normal(jax.random.fold_in(random_seed_key, 1), (SEQUENCE_TOKENS, KEY_VALUE_HEADS * HEAD_WIDTH), jnp.float32), -5.0, 5.0)
    keys_base = gaussian_keys
    random_jitter = 0.05 * jax.random.normal(jax.random.fold_in(random_seed_key, 3), (SEQUENCE_TOKENS, KEY_VALUE_HEADS * HEAD_WIDTH), jnp.float32)
    next_keys = jnp.roll(keys_base, -1, axis=0)
    next_factor = jnp.roll(1.0 - 0.18 / levels, -1)
    next_chosen = jnp.roll(chosen, -1)
    near_keys = jnp.clip(next_factor[:, None] * next_keys + random_jitter, -6.0, 6.0)
    keys_final = jnp.where(next_chosen[:, None], near_keys, keys_base)
    normal_query = jnp.clip(jax.random.normal(jax.random.fold_in(random_seed_key, 5), (SEQUENCE_TOKENS, QUERY_HEADS * HEAD_WIDTH), jnp.float32), -5.0, 5.0)
    query_base = normal_query
    key_rounded_copy = keys_final.astype(jnp.bfloat16).astype(jnp.float32)
    widened_keys = jnp.broadcast_to(key_rounded_copy.reshape(SEQUENCE_TOKENS, KEY_VALUE_HEADS, 1, HEAD_WIDTH), (SEQUENCE_TOKENS, KEY_VALUE_HEADS, QUERY_HEADS // KEY_VALUE_HEADS, HEAD_WIDTH)).reshape(SEQUENCE_TOKENS, QUERY_HEADS * HEAD_WIDTH)
    query_final = jnp.where(chosen[:, None], levels[:, None] * widened_keys, query_base)
    return (keys_final, query_final)


def draw_span_map(key, part):
    span_table, starts = layout(key)
    return span_table


def draw_doc_starts(key, part):
    span_table, starts = layout(key)
    return starts


def draw_key_head_states(key, part):
    keys_final, query_final = fields(key, 0.0)
    return keys_final.astype(jnp.bfloat16)


def draw_queries(key, part):
    keys_final, query_final = fields(key, 0.0)
    return query_final.astype(jnp.bfloat16)


def block_levels(stream_key, shape, pieces, smallest, top_value):
    factor_of = 1.0
    for dim, shards_of in pieces:
        heights = jax.random.uniform(jax.random.fold_in(jax.random.fold_in(stream_key, 6), dim), (shards_of,), jnp.float32, smallest / len(pieces), top_value / len(pieces))
        factor_of = factor_of * jnp.repeat(jnp.exp(heights), shape[dim] // shards_of).reshape((-1,) + (1,) * (len(shape) - 1 - dim))
    return factor_of


def noise(own_key, dims, scale, reach, shards=(), kind=jnp.bfloat16):
    values = scale * jax.random.normal(own_key, dims, jnp.float32)
    if shards:
        values = values * block_levels(own_key, dims, shards, -0.22, 0.18)
    return jnp.clip(values, -reach, reach).astype(kind)


def setup_inputs(seed: int = 0) -> dict:
    splits = jax.random.split(jax.random.key(seed), 7)
    return {
        "queries": draw_queries(jax.random.fold_in(splits[6], 71), 0),
        "key_head_states": draw_key_head_states(jax.random.fold_in(splits[6], 71), 0),
        "value_head_states": noise(splits[2], (SEQUENCE_TOKENS, KEY_VALUE_HEADS * HEAD_WIDTH), 1.0, 6.0, ((0, 256),)),
        "output_gradient": noise(splits[3], (SEQUENCE_TOKENS, QUERY_HEADS * HEAD_WIDTH), 1.0, 6.0, ((0, 256),)),
        "doc_starts": draw_doc_starts(jax.random.fold_in(splits[6], 71), 0),
        "span_map": draw_span_map(jax.random.fold_in(splits[6], 71), 0),
    }


def doc_number(positions, doc_starts):
    covered = (positions[:, None] >= doc_starts[None, :]).astype(jnp.int32)
    return jnp.sum(covered, axis=1) - 1


def reference(queries, key_head_states, value_head_states, output_gradient, doc_starts, span_map):
    query_group_count = QUERY_HEADS // KEY_VALUE_HEADS
    softmax_scale = 1.0 / (HEAD_WIDTH ** 0.5)
    row_ids = jnp.arange(SEQUENCE_TOKENS, dtype=jnp.int32)
    row_pos = (span_map[row_ids // SPAN] * SPAN + row_ids % SPAN).astype(jnp.int32)
    slot_of_span = jnp.argsort(span_map).astype(jnp.int32)
    row_for_position = (slot_of_span[row_ids // SPAN] * SPAN + row_ids % SPAN).astype(jnp.int32)
    query_global = queries[row_for_position].astype(jnp.float32).reshape(SEQUENCE_TOKENS, KEY_VALUE_HEADS, query_group_count, HEAD_WIDTH)
    gradient_global = output_gradient[row_for_position].astype(jnp.float32).reshape(SEQUENCE_TOKENS, KEY_VALUE_HEADS, query_group_count, HEAD_WIDTH)
    key_global = key_head_states[row_for_position].astype(jnp.float32).reshape(SEQUENCE_TOKENS, KEY_VALUE_HEADS, HEAD_WIDTH)
    value_global = value_head_states[row_for_position].astype(jnp.float32).reshape(SEQUENCE_TOKENS, KEY_VALUE_HEADS, HEAD_WIDTH)
    key_doc = doc_number(row_ids, doc_starts)
    block_rows = min(256, SEQUENCE_TOKENS)
    window = min(SEQUENCE_TOKENS, SEQUENCE_TOKENS // 4 + block_rows)

    def block_step(carry, block_id):
        key_gradient_sum, value_gradient_sum = carry
        block_begin = (block_id * block_rows).astype(jnp.int32)
        win_begin = jnp.clip(block_begin - SEQUENCE_TOKENS // 4, 0, SEQUENCE_TOKENS - window).astype(jnp.int32)
        query_rows = lax.dynamic_slice_in_dim(query_global, block_begin, block_rows, 0)
        grad_rows = lax.dynamic_slice_in_dim(gradient_global, block_begin, block_rows, 0)
        query_pos = block_begin + jnp.arange(block_rows, dtype=jnp.int32)
        query_doc = lax.dynamic_slice_in_dim(key_doc, block_begin, block_rows, 0)
        key_block = lax.dynamic_slice_in_dim(key_global, win_begin, window, 0)
        value_block = lax.dynamic_slice_in_dim(value_global, win_begin, window, 0)
        key_pos = win_begin + jnp.arange(window, dtype=jnp.int32)
        block_doc = lax.dynamic_slice_in_dim(key_doc, win_begin, window, 0)
        scores = jnp.einsum("tgjd,kgd->tgjk", query_rows, key_block) * softmax_scale
        same_doc = (query_doc[:, None] == block_doc[None, :]) & (key_pos[None, :] <= query_pos[:, None])
        allowed = same_doc[:, None, None, :]
        masked = jnp.where(allowed, scores, -jnp.inf)
        row_max = jnp.max(masked, axis=-1, keepdims=True)
        row_sum = jnp.sum(jnp.where(allowed, jnp.exp(masked - row_max), 0.0), axis=-1, keepdims=True)
        log_total = row_max + jnp.log(row_sum)
        weights = jnp.where(allowed, jnp.exp(scores - log_total), 0.0)
        dweights = jnp.einsum("tgjd,kgd->tgjk", grad_rows, value_block)
        row_delta = jnp.sum(weights * dweights, axis=-1, keepdims=True)
        dscores = weights * (dweights - row_delta)
        weights_b = lax.optimization_barrier(weights.astype(jnp.bfloat16)).astype(jnp.float32)
        dscores_b = lax.optimization_barrier(dscores.astype(jnp.bfloat16)).astype(jnp.float32)
        query_block_grad = (softmax_scale * jnp.einsum("tgjk,kgd->tgjd", dscores_b, key_block)).astype(jnp.bfloat16)
        key_part = jnp.einsum("tgjk,tgjd->kgd", dscores_b, query_rows)
        value_part = jnp.einsum("tgjk,tgjd->kgd", weights_b, grad_rows)
        key_gradient_sum = lax.dynamic_update_slice_in_dim(key_gradient_sum, lax.dynamic_slice_in_dim(key_gradient_sum, win_begin, window, 0) + key_part, win_begin, 0)
        value_gradient_sum = lax.dynamic_update_slice_in_dim(value_gradient_sum, lax.dynamic_slice_in_dim(value_gradient_sum, win_begin, window, 0) + value_part, win_begin, 0)
        return (key_gradient_sum, value_gradient_sum), query_block_grad

    initial_state = (jnp.zeros((SEQUENCE_TOKENS, KEY_VALUE_HEADS, HEAD_WIDTH), jnp.float32), jnp.zeros((SEQUENCE_TOKENS, KEY_VALUE_HEADS, HEAD_WIDTH), jnp.float32))
    (key_gradient_sum, value_gradient_sum), query_blocks = lax.scan(block_step, initial_state, jnp.arange(SEQUENCE_TOKENS // block_rows, dtype=jnp.int32))
    query_grad_glob = query_blocks.reshape(SEQUENCE_TOKENS, QUERY_HEADS * HEAD_WIDTH)
    key_gradient_global = (softmax_scale * key_gradient_sum).reshape(SEQUENCE_TOKENS, KEY_VALUE_HEADS * HEAD_WIDTH)
    value_gradient_global = value_gradient_sum.reshape(SEQUENCE_TOKENS, KEY_VALUE_HEADS * HEAD_WIDTH)
    return (query_grad_glob[row_pos], key_gradient_global[row_pos].astype(jnp.bfloat16), value_gradient_global[row_pos].astype(jnp.bfloat16))
```

```python
import math

import jax
import jax.numpy as jnp
from jax import lax
from jax.experimental import pallas as pl
from jax.experimental.pallas import tpu as pltpu
from jax.sharding import PartitionSpec as P

MESH = pl.DeviceIdType.MESH
HEADS = 8
WIDTH = 128
ROWS = 32
PEERS = 8
RING = 8
SPAN = 64
KEYS = 4096
BLOCK = 256
STRETCH = 2048
SCALE = 1.0 / math.sqrt(WIDTH)
SCALE_LOG2 = SCALE * math.log2(math.e)
NEG_BIG = -1e30


def place():
    c, t = lax.axis_index("ctx"), lax.axis_index("tp")
    return c // PEERS, c % PEERS, t, t // 2, t % 2


def peer_of(p, d):
    return ((p // 4 + d // 4) % 2) * 4 + (p % 4 + d % 4) % 4


def greet(z, p, t, right, left, sibling):
    barrier = pltpu.get_barrier_semaphore()
    targets = [(z * PEERS + peer_of(p, d), t) for d in range(1, PEERS)]
    targets += [(right, t), (left, t), (z * PEERS + p, sibling)]
    for target in targets:
        pl.semaphore_signal(barrier, inc=1, device_id=target, device_id_type=MESH)
    pl.semaphore_wait(barrier, len(targets))


def remote(src, dst, send, recv, target):
    copy = pltpu.make_async_remote_copy(
        src_ref=src, dst_ref=dst, send_sem=send, recv_sem=recv, device_id=target, device_id_type=MESH
    )
    copy.start()
    return copy


def gather_kernel(
    q, do, k, v, qg, dog, kv, kv_s, kv_r, q_s, q_r, ring_s, ring_r, sib_s, sib_r
):
    z, p, t, y_lo, core = place()
    right, left = ((z + 1) % RING) * PEERS + p, ((z + RING - 1) % RING) * PEERS + p
    here = z * PEERS + p
    sibling = y_lo * 2 + 1 - core
    greet(z, p, t, right, left, sibling)
    small, large, ring, across = [], [], {}, []
    for d in range(1, PEERS):
        other = peer_of(p, d)
        for part, src in enumerate((k, v)):
            small.append(
                remote(
                    src.at[:, pl.ds(pl.multiple_of(other * WIDTH, WIDTH), WIDTH)],
                    kv.at[core, z, part, pl.ds(p * ROWS, ROWS)],
                    kv_s.at[d, part],
                    kv_r.at[d, part],
                    (z * PEERS + other, t),
                )
            )
    own = []
    for part, src in enumerate((k, v)):
        copy = pltpu.make_async_copy(
            src.at[:, pl.ds(pl.multiple_of(p * WIDTH, WIDTH), WIDTH)],
            kv.at[core, z, part, pl.ds(p * ROWS, ROWS)],
            kv_s.at[0, part],
        )
        copy.start()
        own.append(copy)
    wide = HEADS * WIDTH
    for d in range(1, PEERS):
        other = peer_of(p, d)
        for part, (src, dst) in enumerate(((q, qg), (do, dog))):
            large.append(
                remote(
                    src.at[:, pl.ds(pl.multiple_of(other * wide, wide), wide)],
                    dst.at[p],
                    q_s.at[d, part],
                    q_r.at[d, part],
                    (z * PEERS + other, t),
                )
            )
    own_large = []
    for part, (src, dst) in enumerate(((q, qg), (do, dog))):
        copy = pltpu.make_async_copy(
            src.at[:, pl.ds(pl.multiple_of(p * wide, wide), wide)], dst.at[p], q_s.at[0, part]
        )
        copy.start()
        own_large.append(copy)
    for copy in own:
        copy.wait()
    for copy in small:
        copy.wait_recv()

    def forward(step, way, part, offset):
        chunk = kv.at[core, (z + offset) % RING, part]
        target = (right if way == 0 else left, t)
        ring[step, way, part] = remote(
            chunk, chunk, ring_s.at[step, way, part], ring_r.at[step, way, part], target
        )

    def share(part, offset):
        chunk = kv.at[core, (z + offset) % RING, part]
        across.append(
            remote(chunk, chunk, sib_s.at[offset, part], sib_r.at[offset, part], (here, sibling))
        )

    for part in range(2):
        for way in range(2):
            forward(0, way, part, 0)
    for part in range(2):
        share(part, 0)
    for step in range(1, 5):
        for part in range(2):
            for way in range(2):
                if step == 4 and way != part:
                    continue
                offset = RING - step if way == 0 else step
                ring[step - 1, way, part].wait_recv()
                if step < 3 or (step == 3 and way == part):
                    forward(step, way, part, offset)
                share(part, offset)
    for copy in across:
        copy.wait_recv()
    for copy in large:
        copy.wait()
    for copy in own_large:
        copy.wait()
    for copy in small + list(ring.values()) + across:
        copy.wait_send()


def attention_kernel(
    spans, starts, q, do, kv, dq, dkv, key, value, key_t, dkey, dvalue, scores, dweights, dq_t
):
    z, p, t, y_lo, core = place()
    del p, t
    base = y_lo * KEYS

    def local_row(c, half):
        return pl.multiple_of(spans[2 * c + y_lo] * SPAN - base + half * ROWS, ROWS)

    def place_keys(i, _):
        for half in range(2):
            row = local_row(i, half)
            slot = pl.multiple_of((i % PEERS) * ROWS, ROWS)
            key[pl.ds(row, ROWS)] = kv[half, i // PEERS, 0, pl.ds(slot, ROWS)]
            value[pl.ds(row, ROWS)] = kv[half, i // PEERS, 1, pl.ds(slot, ROWS)]
        return 0

    lax.fori_loop(0, RING * PEERS, place_keys, 0)

    def turn_keys(b, _):
        rows = pl.ds(pl.multiple_of(b * BLOCK, BLOCK), BLOCK)
        key_t[b] = key[rows].T
        dkey[rows] = jnp.zeros((BLOCK, WIDTH), jnp.float32)
        dvalue[rows] = jnp.zeros((BLOCK, WIDTH), jnp.float32)
        return 0

    lax.fori_loop(0, KEYS // BLOCK, turn_keys, 0)
    columns = HEADS * ROWS

    def tile(i, _):
        first = local_row(z * PEERS + i, core)
        queries = jnp.concatenate(
            [q[i, :, h * WIDTH : (h + 1) * WIDTH] for h in range(HEADS)], axis=0
        )
        grads = jnp.concatenate(
            [do[i, :, h * WIDTH : (h + 1) * WIDTH] for h in range(HEADS)], axis=0
        )
        row = first + lax.broadcasted_iota(jnp.int32, (1, columns), 1) % ROWS
        begin = jnp.int32(0)
        low = jnp.zeros((1, columns), jnp.int32)
        for n in range(starts.shape[0]):
            start = starts[n] - base
            begin = jnp.where(start <= first, jnp.maximum(begin, start), begin)
            low = jnp.where(start <= row, jnp.maximum(low, start), low)
        begin_block = begin // BLOCK
        end_block = (first + ROWS - 1) // BLOCK + 1

        def score_step(b, top):
            rows = pl.ds(pl.multiple_of(b * BLOCK, BLOCK), BLOCK)
            here = pl.ds(pl.multiple_of((b % (STRETCH // BLOCK)) * BLOCK, BLOCK), BLOCK)
            s = lax.dot_general(
                key[rows], queries, (((1,), (1,)), ((), ())), preferred_element_type=jnp.float32
            )
            dweights[here] = lax.dot_general(
                value[rows], grads, (((1,), (1,)), ((), ())), preferred_element_type=jnp.float32
            )
            pos = b * BLOCK + lax.broadcasted_iota(jnp.int32, (BLOCK, columns), 0)
            s = jnp.where((pos >= low) & (pos <= row), s * SCALE_LOG2, NEG_BIG)
            scores[here] = s
            return jnp.maximum(top, jnp.max(s.reshape(BLOCK // 8, 8, columns), axis=0))

        top = lax.fori_loop(
            begin_block, end_block, score_step, jnp.full((8, columns), NEG_BIG, jnp.float32)
        )
        top = jnp.max(top, axis=0, keepdims=True)

        def sum_step(b, carry):
            total, dot = carry
            here = pl.ds(pl.multiple_of((b % (STRETCH // BLOCK)) * BLOCK, BLOCK), BLOCK)
            e = jnp.exp2(scores[here] - top)
            scores[here] = e
            total += jnp.sum(e.reshape(BLOCK // 8, 8, columns), axis=0)
            dot += jnp.sum((e * dweights[here]).reshape(BLOCK // 8, 8, columns), axis=0)
            return total, dot

        zero = jnp.zeros((8, columns), jnp.float32)
        total, dot = lax.fori_loop(begin_block, end_block, sum_step, (zero, zero))
        inverse = 1.0 / jnp.sum(total, axis=0, keepdims=True)
        delta = jnp.sum(dot, axis=0, keepdims=True) * inverse
        dq_t[...] = jnp.zeros_like(dq_t)

        def grad_step(b, _):
            rows = pl.ds(pl.multiple_of(b * BLOCK, BLOCK), BLOCK)
            here = pl.ds(pl.multiple_of((b % (STRETCH // BLOCK)) * BLOCK, BLOCK), BLOCK)
            w = scores[here] * inverse
            ds = (w * (dweights[here] - delta)).astype(jnp.bfloat16)
            dvalue[rows] += jnp.dot(
                w.astype(jnp.bfloat16), grads, preferred_element_type=jnp.float32
            )
            dkey[rows] += jnp.dot(ds, queries, preferred_element_type=jnp.float32)
            dq_t[...] += jnp.dot(key_t[b], ds, preferred_element_type=jnp.float32)
            return 0

        lax.fori_loop(begin_block, end_block, grad_step, 0)
        out = (dq_t[...] * SCALE).T.astype(jnp.bfloat16)
        for h in range(HEADS):
            dq[i, :, h * WIDTH : (h + 1) * WIDTH] = out[h * ROWS : (h + 1) * ROWS]
        return 0

    lax.fori_loop(0, PEERS, tile, 0)

    def give_keys(i, _):
        for half in range(2):
            row = local_row(i, half)
            slot = pl.multiple_of((i % PEERS) * ROWS, ROWS)
            dkv[half, i // PEERS, 0, pl.ds(slot, ROWS)] = (dkey[pl.ds(row, ROWS)] * SCALE).astype(
                jnp.bfloat16
            )
            dkv[half, i // PEERS, 1, pl.ds(slot, ROWS)] = dvalue[pl.ds(row, ROWS)].astype(
                jnp.bfloat16
            )
        return 0

    lax.fori_loop(0, RING * PEERS, give_keys, 0)


def scatter_kernel(
    dqp, dkv, dq, dk, dv, own, pair, got, sent, final,
    own_s, pair_s, pair_r, q_s, q_r, ring_s, ring_r, kv_s, kv_r,
):
    z, p, t, y_lo, core = place()
    right, left = ((z + 1) % RING) * PEERS + p, ((z + RING - 1) % RING) * PEERS + p
    here = z * PEERS + p
    sibling = y_lo * 2 + 1 - core
    order = (4, 3, 5, 2, 6, 1, 7, 0)
    loads, across, large, ring, small = {}, {}, [], {}, []
    for offset in order:
        copy = pltpu.make_async_copy(
            dkv.at[core, (z + offset) % RING], own.at[offset], own_s.at[offset]
        )
        copy.start()
        loads[offset] = copy
    greet(z, p, t, right, left, sibling)
    for offset in order:
        across[offset] = remote(
            dkv.at[1 - core, (z + offset) % RING],
            pair.at[offset],
            pair_s.at[offset],
            pair_r.at[offset],
            (here, sibling),
        )
    wide = HEADS * WIDTH
    columns = pl.ds(pl.multiple_of(p * wide, wide), wide)
    for d in range(1, PEERS):
        other = peer_of(p, d)
        large.append(
            remote(
                dqp.at[other], dq.at[:, columns], q_s.at[d], q_r.at[d], (z * PEERS + other, t)
            )
        )
    own_large = pltpu.make_async_copy(dqp.at[p], dq.at[:, columns], q_s.at[0])
    own_large.start()

    def term(offset, part):
        return own[offset, part].astype(jnp.float32) + pair[offset, part].astype(jnp.float32)

    for step in range(4):
        for way in range(2):
            offset = 4 - step if way == 0 else 4 + step
            if offset in loads:
                loads.pop(offset).wait()
                across[offset].wait_recv()
            for part in range(2):
                if step == 0 and part != way:
                    continue
                value = term(offset, part)
                if step > 1 or (step == 1 and part == way):
                    ring[step - 1, way, part].wait_recv()
                    value += got[step - 1, way, part].astype(jnp.float32)
                sent[step, way, part] = value.astype(jnp.bfloat16)
                ring[step, way, part] = remote(
                    sent.at[step, way, part],
                    got.at[step, way, part],
                    ring_s.at[step, way, part],
                    ring_r.at[step, way, part],
                    (right if way == 0 else left, t),
                )
    loads.pop(0).wait()
    across[0].wait_recv()
    narrow = pl.ds(pl.multiple_of(p * WIDTH, WIDTH), WIDTH)
    own_small = []
    for part, dst in enumerate((dk, dv)):
        value = term(0, part)
        for way in range(2):
            ring[3, way, part].wait_recv()
            value += got[3, way, part].astype(jnp.float32)
        final[part] = value.astype(jnp.bfloat16)
        for d in range(1, PEERS):
            other = peer_of(p, d)
            small.append(
                remote(
                    final.at[part, pl.ds(other * ROWS, ROWS)],
                    dst.at[:, narrow],
                    kv_s.at[d, part],
                    kv_r.at[d, part],
                    (z * PEERS + other, t),
                )
            )
        copy = pltpu.make_async_copy(
            final.at[part, pl.ds(p * ROWS, ROWS)], dst.at[:, narrow], kv_s.at[0, part]
        )
        copy.start()
        own_small.append(copy)
    for copy in large + small:
        copy.wait()
    for copy in [own_large] + own_small:
        copy.wait()
    for copy in list(ring.values()) + list(across.values()):
        copy.wait_send()


def shards(queries, key_head_states, value_head_states, output_gradient, doc_starts, span_map):
    anywhere = pl.BlockSpec(memory_space=pl.ANY)
    vmem = pl.BlockSpec(memory_space=pltpu.VMEM)
    smem = pl.BlockSpec(memory_space=pltpu.SMEM)
    dma = pltpu.SemaphoreType.DMA
    b16, f32 = jnp.bfloat16, jnp.float32
    wide = HEADS * WIDTH
    rows = PEERS * ROWS
    grouped = jax.ShapeDtypeStruct((PEERS, ROWS, wide), b16)
    chunks = jax.ShapeDtypeStruct((2, RING, 2, rows, WIDTH), b16)
    qg, dog, kv = pl.pallas_call(
        gather_kernel,
        out_shape=(grouped, grouped, chunks),
        in_specs=[anywhere] * 4,
        out_specs=(anywhere,) * 3,
        scratch_shapes=[
            dma((PEERS, 2)),
            dma((PEERS, 2)),
            dma((PEERS, 2)),
            dma((PEERS, 2)),
            dma((4, 2, 2)),
            dma((4, 2, 2)),
            dma((RING, 2)),
            dma((RING, 2)),
        ],
        compiler_params=pltpu.CompilerParams(collective_id=0, has_side_effects=True),
        name="gather_heads",
    )(queries, output_gradient, key_head_states, value_head_states)
    dqp, dkv = pl.pallas_call(
        attention_kernel,
        out_shape=(grouped, chunks),
        in_specs=[smem, smem, vmem, vmem, vmem],
        out_specs=(vmem, vmem),
        scratch_shapes=[
            pltpu.VMEM((KEYS, WIDTH), b16),
            pltpu.VMEM((KEYS, WIDTH), b16),
            pltpu.VMEM((KEYS // BLOCK, WIDTH, BLOCK), b16),
            pltpu.VMEM((KEYS, WIDTH), f32),
            pltpu.VMEM((KEYS, WIDTH), f32),
            pltpu.VMEM((STRETCH, HEADS * ROWS), f32),
            pltpu.VMEM((STRETCH, HEADS * ROWS), f32),
            pltpu.VMEM((WIDTH, HEADS * ROWS), f32),
        ],
        compiler_params=pltpu.CompilerParams(vmem_limit_bytes=48 * 1024 * 1024),
        name="attention_grads",
    )(span_map, doc_starts, qg, dog, kv)
    return pl.pallas_call(
        scatter_kernel,
        out_shape=(
            jax.ShapeDtypeStruct((ROWS, PEERS * wide), b16),
            jax.ShapeDtypeStruct((ROWS, PEERS * WIDTH), b16),
            jax.ShapeDtypeStruct((ROWS, PEERS * WIDTH), b16),
        ),
        in_specs=[anywhere] * 2,
        out_specs=(anywhere,) * 3,
        scratch_shapes=[
            pltpu.VMEM((RING, 2, rows, WIDTH), b16),
            pltpu.VMEM((RING, 2, rows, WIDTH), b16),
            pltpu.VMEM((4, 2, 2, rows, WIDTH), b16),
            pltpu.VMEM((4, 2, 2, rows, WIDTH), b16),
            pltpu.VMEM((2, rows, WIDTH), b16),
            dma((RING,)),
            dma((RING,)),
            dma((RING,)),
            dma((PEERS,)),
            dma((PEERS,)),
            dma((4, 2, 2)),
            dma((4, 2, 2)),
            dma((PEERS, 2)),
            dma((PEERS, 2)),
        ],
        compiler_params=pltpu.CompilerParams(
            collective_id=1, has_side_effects=True, vmem_limit_bytes=32 * 1024 * 1024
        ),
        name="scatter_grads",
    )(dqp, dkv)


def solution(mesh):
    rows = P(("ctx", "tp"), None)
    in_specs = (rows, rows, rows, rows, P(), P())
    return jax.shard_map(
        shards, mesh=mesh, in_specs=in_specs, out_specs=(rows, rows, rows), check_vma=False
    )
```

```python
import math

import jax
import jax.numpy as jnp
from jax import lax
from jax.experimental import pallas as pl
from jax.experimental.pallas import tpu as pltpu
from jax.sharding import PartitionSpec as P

MESH = pl.DeviceIdType.MESH
ORDER = (1, 3, 2, 4, 5, 7, 6)
HEADS = 8
WIDTH = 128
ROWS = 32
PEERS = 8
RING = 8
SPAN = 64
KEYS = 4096
BLOCK = 512
STRETCH = 2048
SCALE = 1.0 / math.sqrt(WIDTH)
SCALE_LOG2 = SCALE * math.log2(math.e)
NEG_BIG = -1e30


def place():
    c, t = lax.axis_index("ctx"), lax.axis_index("tp")
    return c // PEERS, c % PEERS, t, t // 2, t % 2


def peer_of(p, d):
    return ((p // 4 + d // 4) % 2) * 4 + (p % 4 + d % 4) % 4


def half_rows(p, half):
    rows = PEERS * ROWS // 2
    return pl.ds(pl.multiple_of(((p // 4 + half) % 2) * rows, rows), rows)


def greet(z, p, t, right, left, sibling):
    barrier = pltpu.get_barrier_semaphore()
    targets = [(z * PEERS + peer_of(p, d), t) for d in range(1, PEERS)]
    targets += [(right, t), (left, t), (z * PEERS + p, sibling)]
    for target in targets:
        pl.semaphore_signal(barrier, inc=1, device_id=target, device_id_type=MESH)
    pl.semaphore_wait(barrier, len(targets))


def remote(src, dst, send, recv, target):
    copy = pltpu.make_async_remote_copy(
        src_ref=src, dst_ref=dst, send_sem=send, recv_sem=recv, device_id=target, device_id_type=MESH
    )
    copy.start()
    return copy


def gather_kernel(
    q, do, k, v, qg, dog, kv, kv_s, kv_r, q_s, q_r, ring_s, ring_r, sib_s, sib_r
):
    z, p, t, y_lo, core = place()
    right, left = ((z + 1) % RING) * PEERS + p, ((z + RING - 1) % RING) * PEERS + p
    here = z * PEERS + p
    sibling = y_lo * 2 + 1 - core
    greet(z, p, t, right, left, sibling)
    small, large, ring, across, own = {}, [], {}, [], []
    for part, src in enumerate((k, v)):
        copy = pltpu.make_async_copy(
            src.at[:, pl.ds(pl.multiple_of(p * WIDTH, WIDTH), WIDTH)],
            kv.at[core, z, part, pl.ds(p * ROWS, ROWS)],
            kv_s.at[0, part],
        )
        copy.start()
        own.append(copy)
    for d in ORDER:
        other = peer_of(p, d)
        for part, src in enumerate((k, v)):
            small[d, part] = remote(
                src.at[:, pl.ds(pl.multiple_of(other * WIDTH, WIDTH), WIDTH)],
                kv.at[core, z, part, pl.ds(p * ROWS, ROWS)],
                kv_s.at[d, part],
                kv_r.at[d, part],
                (z * PEERS + other, t),
            )
    wide = HEADS * WIDTH
    for d in ORDER:
        other = peer_of(p, d)
        for part, (src, dst) in enumerate(((q, qg), (do, dog))):
            large.append(
                remote(
                    src.at[:, pl.ds(pl.multiple_of(other * wide, wide), wide)],
                    dst.at[p],
                    q_s.at[d, part],
                    q_r.at[d, part],
                    (z * PEERS + other, t),
                )
            )
    own_large = []
    for part, (src, dst) in enumerate(((q, qg), (do, dog))):
        copy = pltpu.make_async_copy(
            src.at[:, pl.ds(pl.multiple_of(p * wide, wide), wide)], dst.at[p], q_s.at[0, part]
        )
        copy.start()
        own_large.append(copy)

    def piece(part, half, offset):
        return kv.at[core, (z + offset) % RING, part, half_rows(p, half)]

    def forward(step, way, part, half, offset):
        chunk = piece(part, half, offset)
        key = step, way, part, half
        target = (right if way == 0 else left, t)
        ring[key] = remote(chunk, chunk, ring_s.at[key], ring_r.at[key], target)

    def share(part, half, offset):
        chunk = piece(part, half, offset)
        key = offset, part, half
        across.append(remote(chunk, chunk, sib_s.at[key], sib_r.at[key], (here, sibling)))

    for half in range(2):
        for part in range(2):
            if half == 0:
                own[part].wait()
            for d in ORDER:
                if d // 4 == half:
                    small[d, part].wait_recv()
            for way in range(2):
                forward(0, way, part, half, 0)
            share(part, half, 0)
    for step in range(1, 5):
        for half in range(2):
            for part in range(2):
                for way in range(2):
                    if step == 4 and way != part:
                        continue
                    offset = RING - step if way == 0 else step
                    ring[step - 1, way, part, half].wait_recv()
                    if step < 3 or (step == 3 and way == part):
                        forward(step, way, part, half, offset)
                    share(part, half, offset)
    for copy in across:
        copy.wait_recv()
    for copy in large:
        copy.wait()
    for copy in own_large:
        copy.wait()
    for copy in list(small.values()) + list(ring.values()) + across:
        copy.wait_send()


def attention_kernel(
    spans_in, starts_in, q, do, kv, dq, dkv,
    spans, starts, key, value, key_t, dkey, dvalue, powers, dweights, tops, dq_t, sems,
):
    loads = [
        pltpu.make_async_copy(spans_in, spans, sems.at[0]),
        pltpu.make_async_copy(starts_in, starts, sems.at[1]),
    ]
    for copy in loads:
        copy.start()
    z, p, t, y_lo, core = place()
    del p, t
    base = y_lo * KEYS

    def clear(b, _):
        rows = pl.ds(pl.multiple_of(b * BLOCK, BLOCK), BLOCK)
        dkey[rows] = jnp.zeros((BLOCK, WIDTH), jnp.float32)
        dvalue[rows] = jnp.zeros((BLOCK, WIDTH), jnp.float32)
        return 0

    lax.fori_loop(0, KEYS // BLOCK, clear, 0)
    value[KEYS:] = jnp.zeros((BLOCK, WIDTH), jnp.bfloat16)
    key[KEYS:] = jnp.zeros((BLOCK, WIDTH), jnp.bfloat16)
    key_t[:, KEYS:] = jnp.zeros((WIDTH, BLOCK), jnp.bfloat16)
    for copy in loads:
        copy.wait()

    def local_row(c, half):
        return pl.multiple_of(spans[2 * c + y_lo] * SPAN - base + half * ROWS, ROWS)

    def place_keys(i, _):
        for j in range(PEERS):
            for half in range(2):
                row = local_row(i * PEERS + j, half)
                key[pl.ds(row, ROWS)] = kv[half, i, 0, j * ROWS : (j + 1) * ROWS]
                value[pl.ds(row, ROWS)] = kv[half, i, 1, j * ROWS : (j + 1) * ROWS]
        return 0

    lax.fori_loop(0, RING, place_keys, 0)

    def turn_keys(b, _):
        rows = pl.ds(pl.multiple_of(b * BLOCK, BLOCK), BLOCK)
        key_t[:, rows] = key[rows].T
        return 0

    lax.fori_loop(0, KEYS // BLOCK, turn_keys, 0)
    columns = HEADS * ROWS

    def tile(i, _):
        first = local_row(z * PEERS + i, core)
        queries = jnp.concatenate(
            [q[i, :, h * WIDTH : (h + 1) * WIDTH] for h in range(HEADS)], axis=0
        )
        grads = jnp.concatenate(
            [do[i, :, h * WIDTH : (h + 1) * WIDTH] for h in range(HEADS)], axis=0
        )
        row = first + lax.broadcasted_iota(jnp.int32, (1, columns), 1) % ROWS
        begin = jnp.int32(0)
        low = jnp.zeros((1, columns), jnp.int32)
        for n in range(starts.shape[0]):
            start = starts[n] - base
            begin = jnp.where(start <= first, jnp.maximum(begin, start), begin)
            low = jnp.where(start <= row, jnp.maximum(low, start), low)
        begin = (begin // WIDTH) * WIDTH
        steps = (first + ROWS - begin + BLOCK - 1) // BLOCK

        def score_step(b, carry):
            top, total, dot = carry
            here = pl.multiple_of(begin + b * BLOCK, WIDTH)
            rows = pl.ds(here, BLOCK)
            s = lax.dot_general(
                key[rows], queries, (((1,), (1,)), ((), ())), preferred_element_type=jnp.float32
            )
            dw = lax.dot_general(
                value[rows], grads, (((1,), (1,)), ((), ())), preferred_element_type=jnp.float32
            )
            dweights[b] = dw
            pos = here + lax.broadcasted_iota(jnp.int32, (BLOCK, columns), 0)
            s = jnp.where((pos >= low) & (pos <= row), s * SCALE_LOG2, NEG_BIG)
            new = jnp.maximum(top, jnp.max(s, axis=0, keepdims=True))
            e = jnp.exp2(s - new)
            powers[b] = e
            tops[b] = new
            factor = jnp.exp2(top - new)
            total = total * factor + jnp.sum(e, axis=0, keepdims=True)
            dot = dot * factor + jnp.sum(e * dw, axis=0, keepdims=True)
            return new, total, dot

        zero = jnp.zeros((1, columns), jnp.float32)
        top, total, dot = lax.fori_loop(0, steps, score_step, (zero + NEG_BIG, zero, zero))
        inverse = 1.0 / total
        delta = dot * inverse
        dq_t[...] = jnp.zeros_like(dq_t)

        def grad_step(b, _):
            here = pl.multiple_of(begin + b * BLOCK, WIDTH)
            rows = pl.ds(here, BLOCK)
            w = powers[b] * (jnp.exp2(tops[b] - top) * inverse)
            ds = (w * (dweights[b] - delta)).astype(jnp.bfloat16)
            dvalue[rows] += jnp.dot(
                w.astype(jnp.bfloat16), grads, preferred_element_type=jnp.float32
            )
            dkey[rows] += jnp.dot(ds, queries, preferred_element_type=jnp.float32)
            dq_t[...] += jnp.dot(key_t[:, rows], ds, preferred_element_type=jnp.float32)
            return 0

        lax.fori_loop(0, steps, grad_step, 0)
        out = (dq_t[...] * SCALE).T.astype(jnp.bfloat16)
        for h in range(HEADS):
            dq[i, :, h * WIDTH : (h + 1) * WIDTH] = out[h * ROWS : (h + 1) * ROWS]
        return 0

    lax.fori_loop(0, PEERS, tile, 0)

    def give_keys(i, _):
        for j in range(PEERS):
            for half in range(2):
                rows = pl.ds(local_row(i * PEERS + j, half), ROWS)
                slot = slice(j * ROWS, (j + 1) * ROWS)
                dkv[half, i, 0, slot] = (dkey[rows] * SCALE).astype(jnp.bfloat16)
                dkv[half, i, 1, slot] = dvalue[rows].astype(jnp.bfloat16)
        return 0

    lax.fori_loop(0, RING, give_keys, 0)


def scatter_kernel(
    dqp, dkv, dq, dk, dv, pair, got, sent, final,
    pair_s, pair_r, q_s, q_r, ring_s, ring_r, kv_s, kv_r,
):
    z, p, t, y_lo, core = place()
    right, left = ((z + 1) % RING) * PEERS + p, ((z + RING - 1) % RING) * PEERS + p
    here = z * PEERS + p
    sibling = y_lo * 2 + 1 - core
    across, large, ring, small = {}, [], {}, []
    greet(z, p, t, right, left, sibling)
    for offset in (4, 3, 5, 2, 6, 1, 7, 0):
        across[offset] = remote(
            dkv.at[1 - core, (z + offset) % RING],
            pair.at[offset],
            pair_s.at[offset],
            pair_r.at[offset],
            (here, sibling),
        )
    wide = HEADS * WIDTH
    columns = pl.ds(pl.multiple_of(p * wide, wide), wide)
    for d in ORDER:
        other = peer_of(p, d)
        large.append(
            remote(
                dqp.at[other], dq.at[:, columns], q_s.at[d], q_r.at[d], (z * PEERS + other, t)
            )
        )
    own_large = pltpu.make_async_copy(dqp.at[p], dq.at[:, columns], q_s.at[0])
    own_large.start()
    met = set()

    def term(offset, part, half):
        if offset not in met:
            across[offset].wait_recv()
            met.add(offset)
        rows = half_rows(p, half)
        mine = dkv[core, (z + offset) % RING, part, rows].astype(jnp.float32)
        return mine + pair[offset, part, rows].astype(jnp.float32)

    def arrived(step, way, part, half):
        ring[step, way, part, half].wait_recv()
        return got[step, way, part, half_rows(p, half)].astype(jnp.float32)

    for step in range(4):
        for half in (1, 0):
            for part in range(2):
                for way in range(2):
                    if step == 0 and part != way:
                        continue
                    value = term(4 - step if way == 0 else 4 + step, part, half)
                    if step > 1 or (step == 1 and part == way):
                        value += arrived(step - 1, way, part, half)
                    rows = half_rows(p, half)
                    key = step, way, part, half
                    sent[step, way, part, rows] = value.astype(jnp.bfloat16)
                    ring[key] = remote(
                        sent.at[step, way, part, rows],
                        got.at[step, way, part, rows],
                        ring_s.at[key],
                        ring_r.at[key],
                        (right if way == 0 else left, t),
                    )
    narrow = pl.ds(pl.multiple_of(p * WIDTH, WIDTH), WIDTH)
    own_small = []
    for half in (1, 0):
        for part, dst in enumerate((dk, dv)):
            value = term(0, part, half)
            for way in range(2):
                value += arrived(3, way, part, half)
            final[part, half_rows(p, half)] = value.astype(jnp.bfloat16)
            for d in range(PEERS):
                if d // 4 != half:
                    continue
                other = peer_of(p, d)
                src = final.at[part, pl.ds(other * ROWS, ROWS)]
                if d == 0:
                    copy = pltpu.make_async_copy(src, dst.at[:, narrow], kv_s.at[0, part])
                    copy.start()
                    own_small.append(copy)
                else:
                    small.append(
                        remote(
                            src,
                            dst.at[:, narrow],
                            kv_s.at[d, part],
                            kv_r.at[d, part],
                            (z * PEERS + other, t),
                        )
                    )
    for copy in large + small:
        copy.wait()
    for copy in [own_large] + own_small:
        copy.wait()
    for copy in list(ring.values()) + list(across.values()):
        copy.wait_send()


def shards(queries, key_head_states, value_head_states, output_gradient, doc_starts, span_map):
    anywhere = pl.BlockSpec(memory_space=pl.ANY)
    vmem = pl.BlockSpec(memory_space=pltpu.VMEM)
    hbm = pl.BlockSpec(memory_space=pltpu.HBM)
    dma = pltpu.SemaphoreType.DMA
    b16, f32 = jnp.bfloat16, jnp.float32
    wide = HEADS * WIDTH
    rows = PEERS * ROWS
    queries, output_gradient, key_head_states, value_head_states, span_map, doc_starts = (
        pltpu.with_memory_space_constraint(x, pltpu.HBM)
        for x in (queries, output_gradient, key_head_states, value_head_states, span_map, doc_starts)
    )
    grouped = jax.ShapeDtypeStruct((PEERS, ROWS, wide), b16)
    chunks = jax.ShapeDtypeStruct((2, RING, 2, rows, WIDTH), b16)
    qg, dog, kv = pl.pallas_call(
        gather_kernel,
        out_shape=(grouped, grouped, chunks),
        in_specs=[hbm] * 4,
        out_specs=(anywhere,) * 3,
        scratch_shapes=[
            dma((PEERS, 2)),
            dma((PEERS, 2)),
            dma((PEERS, 2)),
            dma((PEERS, 2)),
            dma((4, 2, 2, 2)),
            dma((4, 2, 2, 2)),
            dma((RING, 2, 2)),
            dma((RING, 2, 2)),
        ],
        compiler_params=pltpu.CompilerParams(
            collective_id=0, has_side_effects=True, vmem_limit_bytes=2 * 1024 * 1024
        ),
        name="gather_heads",
    )(queries, output_gradient, key_head_states, value_head_states)
    dqp, dkv = pl.pallas_call(
        attention_kernel,
        out_shape=(grouped, chunks),
        in_specs=[hbm, hbm, vmem, vmem, vmem],
        out_specs=(vmem, vmem),
        scratch_shapes=[
            pltpu.SMEM(span_map.shape, jnp.int32),
            pltpu.SMEM(doc_starts.shape, jnp.int32),
            pltpu.VMEM((KEYS + BLOCK, WIDTH), b16),
            pltpu.VMEM((KEYS + BLOCK, WIDTH), b16),
            pltpu.VMEM((WIDTH, KEYS + BLOCK), b16),
            pltpu.VMEM((KEYS + BLOCK, WIDTH), f32),
            pltpu.VMEM((KEYS + BLOCK, WIDTH), f32),
            pltpu.VMEM((STRETCH // BLOCK, BLOCK, HEADS * ROWS), f32),
            pltpu.VMEM((STRETCH // BLOCK, BLOCK, HEADS * ROWS), f32),
            pltpu.VMEM((STRETCH // BLOCK, 1, HEADS * ROWS), f32),
            pltpu.VMEM((WIDTH, HEADS * ROWS), f32),
            dma((2,)),
        ],
        compiler_params=pltpu.CompilerParams(vmem_limit_bytes=24 * 1024 * 1024),
        name="attention_grads",
    )(span_map, doc_starts, qg, dog, kv)
    return pl.pallas_call(
        scatter_kernel,
        out_shape=(
            jax.ShapeDtypeStruct((ROWS, PEERS * wide), b16),
            jax.ShapeDtypeStruct((ROWS, PEERS * WIDTH), b16),
            jax.ShapeDtypeStruct((ROWS, PEERS * WIDTH), b16),
        ),
        in_specs=[anywhere, vmem],
        out_specs=(anywhere,) * 3,
        scratch_shapes=[
            pltpu.VMEM((RING, 2, rows, WIDTH), b16),
            pltpu.VMEM((4, 2, 2, rows, WIDTH), b16),
            pltpu.VMEM((4, 2, 2, rows, WIDTH), b16),
            pltpu.VMEM((2, rows, WIDTH), b16),
            dma((RING,)),
            dma((RING,)),
            dma((PEERS,)),
            dma((PEERS,)),
            dma((4, 2, 2, 2)),
            dma((4, 2, 2, 2)),
            dma((PEERS, 2)),
            dma((PEERS, 2)),
        ],
        compiler_params=pltpu.CompilerParams(
            collective_id=1, has_side_effects=True, vmem_limit_bytes=12 * 1024 * 1024
        ),
        name="scatter_grads",
    )(dqp, dkv)


def solution(mesh):
    rows = P(("ctx", "tp"), None)
    in_specs = (rows, rows, rows, rows, P(), P())
    return jax.shard_map(
        shards, mesh=mesh, in_specs=in_specs, out_specs=(rows, rows, rows), check_vma=False
    )
```

```python
import math

import jax
import jax.numpy as jnp
from jax import lax
from jax.experimental import pallas as pl
from jax.experimental.pallas import tpu as pltpu
from jax.sharding import PartitionSpec as P

MESH = pl.DeviceIdType.MESH
ORDER = (1, 3, 2, 4, 5, 7, 6)
HEADS = 8
WIDTH = 128
ROWS = 32
PEERS = 8
RING = 8
SPAN = 64
KEYS = 4096
BLOCK = 256
TOGETHER = 6
WORK = PEERS * 2048 // BLOCK
SCALE = 1.0 / math.sqrt(WIDTH)
SCALE_LOG2 = SCALE * math.log2(math.e)
NEG_BIG = -1e30


def place():
    c, t = lax.axis_index("ctx"), lax.axis_index("tp")
    return c // PEERS, c % PEERS, t, t // 2, t % 2


def peer_of(p, d):
    return ((p // 4 + d // 4) % 2) * 4 + (p % 4 + d % 4) % 4


def half_rows(p, half):
    rows = PEERS * ROWS // 2
    return pl.ds(pl.multiple_of(((p // 4 + half) % 2) * rows, rows), rows)


def greet(z, p, t, right, left, sibling):
    barrier = pltpu.get_barrier_semaphore()
    targets = [(z * PEERS + peer_of(p, d), t) for d in range(1, PEERS)]
    targets += [(right, t), (left, t), (z * PEERS + p, sibling)]
    for target in targets:
        pl.semaphore_signal(barrier, inc=1, device_id=target, device_id_type=MESH)
    pl.semaphore_wait(barrier, len(targets))


def remote(src, dst, send, recv, target):
    copy = pltpu.make_async_remote_copy(
        src_ref=src, dst_ref=dst, send_sem=send, recv_sem=recv, device_id=target, device_id_type=MESH
    )
    copy.start()
    return copy


def gather_kernel(
    q, do, k, v, qg, dog, kv, kv_s, kv_r, q_s, q_r, ring_s, ring_r, sib_s, sib_r
):
    z, p, t, y_lo, core = place()
    right, left = ((z + 1) % RING) * PEERS + p, ((z + RING - 1) % RING) * PEERS + p
    here = z * PEERS + p
    sibling = y_lo * 2 + 1 - core
    greet(z, p, t, right, left, sibling)
    small, large, ring, across, own = {}, [], {}, [], []
    for part, src in enumerate((k, v)):
        copy = pltpu.make_async_copy(
            src.at[:, pl.ds(pl.multiple_of(p * WIDTH, WIDTH), WIDTH)],
            kv.at[core, z, part, pl.ds(p * ROWS, ROWS)],
            kv_s.at[0, part],
        )
        copy.start()
        own.append(copy)
    for d in ORDER:
        other = peer_of(p, d)
        for part, src in enumerate((k, v)):
            small[d, part] = remote(
                src.at[:, pl.ds(pl.multiple_of(other * WIDTH, WIDTH), WIDTH)],
                kv.at[core, z, part, pl.ds(p * ROWS, ROWS)],
                kv_s.at[d, part],
                kv_r.at[d, part],
                (z * PEERS + other, t),
            )
    wide = HEADS * WIDTH
    for d in ORDER:
        other = peer_of(p, d)
        for part, (src, dst) in enumerate(((q, qg), (do, dog))):
            large.append(
                remote(
                    src.at[:, pl.ds(pl.multiple_of(other * wide, wide), wide)],
                    dst.at[p],
                    q_s.at[d, part],
                    q_r.at[d, part],
                    (z * PEERS + other, t),
                )
            )
    own_large = []
    for part, (src, dst) in enumerate(((q, qg), (do, dog))):
        copy = pltpu.make_async_copy(
            src.at[:, pl.ds(pl.multiple_of(p * wide, wide), wide)], dst.at[p], q_s.at[0, part]
        )
        copy.start()
        own_large.append(copy)

    def piece(part, half, offset):
        return kv.at[core, (z + offset) % RING, part, half_rows(p, half)]

    def forward(step, way, part, half, offset):
        chunk = piece(part, half, offset)
        key = step, way, part, half
        target = (right if way == 0 else left, t)
        ring[key] = remote(chunk, chunk, ring_s.at[key], ring_r.at[key], target)

    def share(part, half, offset):
        chunk = piece(part, half, offset)
        key = offset, part, half
        across.append(remote(chunk, chunk, sib_s.at[key], sib_r.at[key], (here, sibling)))

    for half in range(2):
        for part in range(2):
            if half == 0:
                own[part].wait()
            for d in ORDER:
                if d // 4 == half:
                    small[d, part].wait_recv()
            for way in range(2):
                forward(0, way, part, half, 0)
            share(part, half, 0)
    for step in range(1, 5):
        for half in range(2):
            for part in range(2):
                for way in range(2):
                    if step == 4 and way != part:
                        continue
                    offset = RING - step if way == 0 else step
                    ring[step - 1, way, part, half].wait_recv()
                    if step < 3 or (step == 3 and way == part):
                        forward(step, way, part, half, offset)
                    share(part, half, offset)
    for copy in across:
        copy.wait_recv()
    for copy in large:
        copy.wait()
    for copy in own_large:
        copy.wait()
    for copy in list(small.values()) + list(ring.values()) + across:
        copy.wait_send()


def attention_kernel(
    spans_in, starts_in, q, do, kv, dq, dkv,
    spans, starts, work_tile, work_row, first_work,
    key, value, dkey, dvalue, queries, grads, lows, highs,
    powers, dweights, tops, totals, dots, tile_top, tile_inverse, tile_delta, dq_sum, sems,
):
    loads = [
        pltpu.make_async_copy(spans_in, spans, sems.at[0]),
        pltpu.make_async_copy(starts_in, starts, sems.at[1]),
    ]
    for copy in loads:
        copy.start()
    z, p, t, y_lo, core = place()
    del p, t
    base = y_lo * KEYS

    def clear(b, _):
        rows = pl.ds(pl.multiple_of(b * BLOCK, BLOCK), BLOCK)
        dkey[rows] = jnp.zeros((BLOCK, WIDTH), jnp.float32)
        dvalue[rows] = jnp.zeros((BLOCK, WIDTH), jnp.float32)
        return 0

    lax.fori_loop(0, KEYS // BLOCK + 1, clear, 0)
    value[KEYS:] = jnp.zeros((BLOCK, WIDTH), jnp.bfloat16)
    key[KEYS:] = jnp.zeros((BLOCK, WIDTH), jnp.bfloat16)
    dq_sum[...] = jnp.zeros_like(dq_sum)
    for i in range(PEERS):
        for h in range(HEADS):
            part = slice(h * WIDTH, (h + 1) * WIDTH)
            queries[i, h * ROWS : (h + 1) * ROWS] = q[i, :, part]
            grads[i, h * ROWS : (h + 1) * ROWS] = do[i, :, part]
    for copy in loads:
        copy.wait()

    def local_row(c, half):
        return pl.multiple_of(spans[2 * c + y_lo] * SPAN - base + half * ROWS, ROWS)

    def place_keys(i, _):
        for j in range(PEERS):
            for half in range(2):
                row = local_row(i * PEERS + j, half)
                key[pl.ds(row, ROWS)] = kv[half, i, 0, j * ROWS : (j + 1) * ROWS]
                value[pl.ds(row, ROWS)] = kv[half, i, 1, j * ROWS : (j + 1) * ROWS]
        return 0

    lax.fori_loop(0, RING, place_keys, 0)

    columns = HEADS * ROWS

    def plan(i, count):
        first = local_row(z * PEERS + i, core)
        row = first + lax.broadcasted_iota(jnp.int32, (1, columns), 1) % ROWS
        begin = jnp.int32(0)
        low = jnp.zeros((1, columns), jnp.int32)
        for n in range(starts.shape[0]):
            start = starts[n] - base
            begin = jnp.where(start <= first, jnp.maximum(begin, start), begin)
            low = jnp.where(start <= row, jnp.maximum(low, start), low)
        lows[i] = low
        highs[i] = row
        begin = (begin // WIDTH) * WIDTH
        steps = (first + ROWS - begin + BLOCK - 1) // BLOCK
        first_work[i] = count

        def enter(b, _):
            work_tile[count + b] = i
            work_row[count + b] = begin + b * BLOCK
            return 0

        lax.fori_loop(0, steps, enter, 0)
        return count + steps

    count = lax.fori_loop(0, PEERS, plan, jnp.int32(0))
    first_work[PEERS] = count
    for u in range(TOGETHER - 1):
        work_tile[count + u] = 0
        work_row[count + u] = KEYS
    groups = (count + TOGETHER - 1) // TOGETHER

    def score_group(g, _):
        products = []
        for u in range(TOGETHER):
            n = g * TOGETHER + u
            i = work_tile[n]
            here = pl.multiple_of(work_row[n], WIDTH)
            rows = pl.ds(here, BLOCK)
            s = lax.dot_general(
                key[rows], queries[i], (((1,), (1,)), ((), ())), preferred_element_type=jnp.float32
            )
            dw = lax.dot_general(
                value[rows], grads[i], (((1,), (1,)), ((), ())), preferred_element_type=jnp.float32
            )
            products.append((here, lows[i], highs[i], s, dw))
        for u, (here, low, high, s, dw) in enumerate(products):
            n = g * TOGETHER + u
            pos = here + lax.broadcasted_iota(jnp.int32, (BLOCK, columns), 0)
            s = jnp.where((pos - low).astype(jnp.uint32) <= (high - low).astype(jnp.uint32), s * SCALE_LOG2, NEG_BIG)
            top = jnp.max(s, axis=0, keepdims=True)
            e = jnp.exp2(s - top)
            dweights[n] = dw
            powers[n] = s
            tops[pl.ds(n, 1)] = top
            totals[pl.ds(n, 1)] = jnp.sum(e, axis=0, keepdims=True)
            dots[pl.ds(n, 1)] = jnp.sum(e * dw, axis=0, keepdims=True)
        return 0

    lax.fori_loop(0, groups, score_group, 0)
    entry = lax.broadcasted_iota(jnp.int32, (WORK, 1), 0)
    for i in range(PEERS):
        mine = (entry >= first_work[i]) & (entry < first_work[i + 1])
        tops_i = jnp.where(mine, tops[:WORK], NEG_BIG)
        top = jnp.max(tops_i, axis=0, keepdims=True)
        factor = jnp.exp2(tops_i - top)
        total = jnp.sum(jnp.where(mine, totals[:WORK] * factor, 0.0), axis=0, keepdims=True)
        dot = jnp.sum(jnp.where(mine, dots[:WORK] * factor, 0.0), axis=0, keepdims=True)
        inverse = 1.0 / total
        tile_top[i] = top + jnp.log2(total)
        tile_inverse[i] = inverse
        tile_delta[i] = dot * inverse

    def grad_group(g, _):
        products = []
        for u in range(TOGETHER):
            n = g * TOGETHER + u
            i = work_tile[n]
            rows = pl.ds(pl.multiple_of(work_row[n], WIDTH), BLOCK)
            w = jnp.exp2(powers[n] - tile_top[i])
            ds = (w * (dweights[n] - tile_delta[i])).astype(jnp.bfloat16)
            w = w.astype(jnp.bfloat16)
            products.append(
                (
                    i,
                    rows,
                    jnp.dot(w, grads[i], preferred_element_type=jnp.float32),
                    jnp.dot(ds, queries[i], preferred_element_type=jnp.float32),
                    lax.dot_general(
                        ds, key[rows], (((0,), (0,)), ((), ())), preferred_element_type=jnp.float32
                    ),
                )
            )
        for i, rows, to_value, to_key, to_query in products:
            dvalue[rows] += to_value
            dkey[rows] += to_key
            dq_sum[i] += to_query
        return 0

    lax.fori_loop(0, groups, grad_group, 0)
    for i in range(PEERS):
        out = (dq_sum[i] * SCALE).astype(jnp.bfloat16)
        for h in range(HEADS):
            dq[i, :, h * WIDTH : (h + 1) * WIDTH] = out[h * ROWS : (h + 1) * ROWS]

    def give_keys(i, _):
        for j in range(PEERS):
            for half in range(2):
                rows = pl.ds(local_row(i * PEERS + j, half), ROWS)
                slot = slice(j * ROWS, (j + 1) * ROWS)
                dkv[half, i, 0, slot] = (dkey[rows] * SCALE).astype(jnp.bfloat16)
                dkv[half, i, 1, slot] = dvalue[rows].astype(jnp.bfloat16)
        return 0

    lax.fori_loop(0, RING, give_keys, 0)


def scatter_kernel(
    dqp, dkv, dq, dk, dv, pair, got, sent, final,
    pair_s, pair_r, q_s, q_r, ring_s, ring_r, kv_s, kv_r,
):
    z, p, t, y_lo, core = place()
    right, left = ((z + 1) % RING) * PEERS + p, ((z + RING - 1) % RING) * PEERS + p
    here = z * PEERS + p
    sibling = y_lo * 2 + 1 - core
    across, large, ring, small = {}, [], {}, []
    greet(z, p, t, right, left, sibling)
    for offset in (4, 3, 5, 2, 6, 1, 7, 0):
        across[offset] = remote(
            dkv.at[1 - core, (z + offset) % RING],
            pair.at[offset],
            pair_s.at[offset],
            pair_r.at[offset],
            (here, sibling),
        )
    wide = HEADS * WIDTH
    columns = pl.ds(pl.multiple_of(p * wide, wide), wide)
    for d in ORDER:
        other = peer_of(p, d)
        large.append(
            remote(
                dqp.at[other], dq.at[:, columns], q_s.at[d], q_r.at[d], (z * PEERS + other, t)
            )
        )
    own_large = pltpu.make_async_copy(dqp.at[p], dq.at[:, columns], q_s.at[0])
    own_large.start()
    met = set()

    def term(offset, part, half):
        if offset not in met:
            across[offset].wait_recv()
            met.add(offset)
        rows = half_rows(p, half)
        mine = dkv[core, (z + offset) % RING, part, rows].astype(jnp.float32)
        return mine + pair[offset, part, rows].astype(jnp.float32)

    def arrived(step, way, part, half):
        ring[step, way, part, half].wait_recv()
        return got[step, way, part, half_rows(p, half)].astype(jnp.float32)

    for step in range(4):
        for half in (1, 0):
            for part in range(2):
                for way in range(2):
                    if step == 0 and part != way:
                        continue
                    value = term(4 - step if way == 0 else 4 + step, part, half)
                    if step > 1 or (step == 1 and part == way):
                        value += arrived(step - 1, way, part, half)
                    rows = half_rows(p, half)
                    key = step, way, part, half
                    sent[step, way, part, rows] = value.astype(jnp.bfloat16)
                    ring[key] = remote(
                        sent.at[step, way, part, rows],
                        got.at[step, way, part, rows],
                        ring_s.at[key],
                        ring_r.at[key],
                        (right if way == 0 else left, t),
                    )
    narrow = pl.ds(pl.multiple_of(p * WIDTH, WIDTH), WIDTH)
    own_small = []
    for half in (1, 0):
        for part, dst in enumerate((dk, dv)):
            value = term(0, part, half)
            for way in range(2):
                value += arrived(3, way, part, half)
            final[part, half_rows(p, half)] = value.astype(jnp.bfloat16)
            for d in range(PEERS):
                if d // 4 != half:
                    continue
                other = peer_of(p, d)
                src = final.at[part, pl.ds(other * ROWS, ROWS)]
                if d == 0:
                    copy = pltpu.make_async_copy(src, dst.at[:, narrow], kv_s.at[0, part])
                    copy.start()
                    own_small.append(copy)
                else:
                    small.append(
                        remote(
                            src,
                            dst.at[:, narrow],
                            kv_s.at[d, part],
                            kv_r.at[d, part],
                            (z * PEERS + other, t),
                        )
                    )
    for copy in large + small:
        copy.wait()
    for copy in [own_large] + own_small:
        copy.wait()
    for copy in list(ring.values()) + list(across.values()):
        copy.wait_send()


def attend(span_map, doc_starts, qg, dog, kv):
    vmem = pl.BlockSpec(memory_space=pltpu.VMEM)
    hbm = pl.BlockSpec(memory_space=pltpu.HBM)
    dma = pltpu.SemaphoreType.DMA
    b16, f32 = jnp.bfloat16, jnp.float32
    columns = HEADS * ROWS
    return pl.pallas_call(
        attention_kernel,
        out_shape=(
            jax.ShapeDtypeStruct(qg.shape, b16),
            jax.ShapeDtypeStruct(kv.shape, b16),
        ),
        in_specs=[hbm, hbm, vmem, vmem, vmem],
        out_specs=(vmem, vmem),
        scratch_shapes=[
            pltpu.SMEM(span_map.shape, jnp.int32),
            pltpu.SMEM(doc_starts.shape, jnp.int32),
            pltpu.SMEM((WORK + TOGETHER,), jnp.int32),
            pltpu.SMEM((WORK + TOGETHER,), jnp.int32),
            pltpu.SMEM((PEERS + 1,), jnp.int32),
            pltpu.VMEM((KEYS + BLOCK, WIDTH), b16),
            pltpu.VMEM((KEYS + BLOCK, WIDTH), b16),
            pltpu.VMEM((KEYS + BLOCK, WIDTH), f32),
            pltpu.VMEM((KEYS + BLOCK, WIDTH), f32),
            pltpu.VMEM((PEERS, columns, WIDTH), b16),
            pltpu.VMEM((PEERS, columns, WIDTH), b16),
            pltpu.VMEM((PEERS, 1, columns), jnp.int32),
            pltpu.VMEM((PEERS, 1, columns), jnp.int32),
            pltpu.VMEM((WORK + TOGETHER, BLOCK, columns), f32),
            pltpu.VMEM((WORK + TOGETHER, BLOCK, columns), f32),
            pltpu.VMEM((WORK + 8, columns), f32),
            pltpu.VMEM((WORK + 8, columns), f32),
            pltpu.VMEM((WORK + 8, columns), f32),
            pltpu.VMEM((PEERS, 1, columns), f32),
            pltpu.VMEM((PEERS, 1, columns), f32),
            pltpu.VMEM((PEERS, 1, columns), f32),
            pltpu.VMEM((PEERS, columns, WIDTH), f32),
            dma((2,)),
        ],
        compiler_params=pltpu.CompilerParams(vmem_limit_bytes=48 * 1024 * 1024),
        name="attention_grads",
    )(span_map, doc_starts, qg, dog, kv)


def gather(queries, output_gradient, key_head_states, value_head_states):
    anywhere = pl.BlockSpec(memory_space=pl.ANY)
    vmem = pl.BlockSpec(memory_space=pltpu.VMEM)
    hbm = pl.BlockSpec(memory_space=pltpu.HBM)
    dma = pltpu.SemaphoreType.DMA
    b16 = jnp.bfloat16
    wide = HEADS * WIDTH
    rows = PEERS * ROWS
    grouped = jax.ShapeDtypeStruct((PEERS, ROWS, wide), b16)
    chunks = jax.ShapeDtypeStruct((2, RING, 2, rows, WIDTH), b16)
    return pl.pallas_call(
        gather_kernel,
        out_shape=(grouped, grouped, chunks),
        in_specs=[hbm] * 4,
        out_specs=(anywhere,) * 3,
        scratch_shapes=[
            dma((PEERS, 2)),
            dma((PEERS, 2)),
            dma((PEERS, 2)),
            dma((PEERS, 2)),
            dma((4, 2, 2, 2)),
            dma((4, 2, 2, 2)),
            dma((RING, 2, 2)),
            dma((RING, 2, 2)),
        ],
        compiler_params=pltpu.CompilerParams(
            collective_id=0, has_side_effects=True, vmem_limit_bytes=2 * 1024 * 1024
        ),
        name="gather_heads",
    )(queries, output_gradient, key_head_states, value_head_states)


def scatter(dqp, dkv):
    anywhere = pl.BlockSpec(memory_space=pl.ANY)
    vmem = pl.BlockSpec(memory_space=pltpu.VMEM)
    hbm = pl.BlockSpec(memory_space=pltpu.HBM)
    dma = pltpu.SemaphoreType.DMA
    b16 = jnp.bfloat16
    wide = HEADS * WIDTH
    rows = PEERS * ROWS
    return pl.pallas_call(
        scatter_kernel,
        out_shape=(
            jax.ShapeDtypeStruct((ROWS, PEERS * wide), b16),
            jax.ShapeDtypeStruct((ROWS, PEERS * WIDTH), b16),
            jax.ShapeDtypeStruct((ROWS, PEERS * WIDTH), b16),
        ),
        in_specs=[anywhere, vmem],
        out_specs=(anywhere,) * 3,
        scratch_shapes=[
            pltpu.VMEM((RING, 2, rows, WIDTH), b16),
            pltpu.VMEM((4, 2, 2, rows, WIDTH), b16),
            pltpu.VMEM((4, 2, 2, rows, WIDTH), b16),
            pltpu.VMEM((2, rows, WIDTH), b16),
            dma((RING,)),
            dma((RING,)),
            dma((PEERS,)),
            dma((PEERS,)),
            dma((4, 2, 2, 2)),
            dma((4, 2, 2, 2)),
            dma((PEERS, 2)),
            dma((PEERS, 2)),
        ],
        compiler_params=pltpu.CompilerParams(
            collective_id=1, has_side_effects=True, vmem_limit_bytes=12 * 1024 * 1024
        ),
        name="scatter_grads",
    )(dqp, dkv)


def finish_kernel(dq_in, dk_in, dv_in, dq, dk, dv, sems):
    copies = [
        pltpu.make_async_copy(src, dst, sems.at[n])
        for n, (src, dst) in enumerate(((dq_in, dq), (dk_in, dk), (dv_in, dv)))
    ]
    for copy in copies:
        copy.start()
    for copy in copies:
        copy.wait()


def finish(*grads):
    anywhere = pl.BlockSpec(memory_space=pl.ANY)
    hbm = pl.BlockSpec(memory_space=pltpu.HBM)
    return pl.pallas_call(
        finish_kernel,
        out_shape=tuple(jax.ShapeDtypeStruct(x.shape, x.dtype) for x in grads),
        in_specs=[anywhere] * 3,
        out_specs=(hbm,) * 3,
        scratch_shapes=[pltpu.SemaphoreType.DMA((3,))],
        compiler_params=pltpu.CompilerParams(vmem_limit_bytes=1024 * 1024),
        name="finish",
    )(*grads)


def shards(queries, key_head_states, value_head_states, output_gradient, doc_starts, span_map):
    queries, output_gradient, key_head_states, value_head_states, span_map, doc_starts = (
        pltpu.with_memory_space_constraint(x, pltpu.HBM)
        for x in (queries, output_gradient, key_head_states, value_head_states, span_map, doc_starts)
    )
    qg, dog, kv = gather(queries, output_gradient, key_head_states, value_head_states)
    dqp, dkv = attend(span_map, doc_starts, qg, dog, kv)
    return finish(*scatter(dqp, dkv))


def solution(mesh):
    rows = P(("ctx", "tp"), None)
    in_specs = (rows, rows, rows, rows, P(), P())
    return jax.shard_map(
        shards, mesh=mesh, in_specs=in_specs, out_specs=(rows, rows, rows), check_vma=False
    )
```

```python
import math

import jax
import jax.numpy as jnp
from jax import lax
from jax.experimental import pallas as pl
from jax.experimental.pallas import tpu as pltpu
from jax.sharding import PartitionSpec as P

MESH = pl.DeviceIdType.MESH
ORDER = (1, 3, 2, 4, 5, 7, 6)
HEADS = 8
WIDTH = 128
ROWS = 32
PEERS = 8
RING = 8
SPAN = 64
KEYS = 4096
BLOCK = 256
TOGETHER = 6
WORK = PEERS * 2048 // BLOCK
SCALE = 1.0 / math.sqrt(WIDTH)
SCALE_LOG2 = SCALE * math.log2(math.e)
NEG_BIG = -1e30


def place():
    c, t = lax.axis_index("ctx"), lax.axis_index("tp")
    return c // PEERS, c % PEERS, t, t // 2, t % 2


def peer_of(p, d):
    return ((p // 4 + d // 4) % 2) * 4 + (p % 4 + d % 4) % 4


def half_rows(p, half):
    rows = PEERS * ROWS // 2
    return pl.ds(pl.multiple_of(((p // 4 + half) % 2) * rows, rows), rows)


def beside(z, p, t, way, far):
    return along_z(z, p, far if way == 0 else RING - far), t


def along_z(z, p, offset):
    return ((z + offset) % RING) * PEERS + p


def greet(z, p, t, sibling, row):
    barrier = pltpu.get_barrier_semaphore()
    targets = [(z * PEERS + peer_of(p, d), t) for d in range(1, PEERS // 2 + 1)]
    targets += [(along_z(z, p, offset), t) for offset in (1, 2, RING - 2, RING - 1)]
    targets.append((z * PEERS + p, sibling))
    for target in targets:
        pl.semaphore_signal(barrier, inc=1, device_id=target, device_id_type=MESH)
    pl.semaphore_wait(barrier, len(targets))
    across = (z * PEERS + peer_of(p, PEERS // 2), t)
    pl.semaphore_signal(row, inc=1, device_id=across, device_id_type=MESH)


def remote(src, dst, send, recv, target):
    copy = pltpu.make_async_remote_copy(
        src_ref=src, dst_ref=dst, send_sem=send, recv_sem=recv, device_id=target, device_id_type=MESH
    )
    copy.start()
    return copy


def gather_kernel(
    q, do, k, v, qg, dog, kv, kv_s, kv_r, q_s, q_r, ring_s, ring_r, sib_s, sib_r, row
):
    z, p, t, y_lo, core = place()
    here = z * PEERS + p
    sibling = y_lo * 2 + 1 - core
    greet(z, p, t, sibling, row)
    small, large, ring, across, own = {}, [], {}, [], []
    for part, src in enumerate((k, v)):
        copy = pltpu.make_async_copy(
            src.at[:, pl.ds(pl.multiple_of(p * WIDTH, WIDTH), WIDTH)],
            kv.at[core, z, part, pl.ds(p * ROWS, ROWS)],
            kv_s.at[0, part],
        )
        copy.start()
        own.append(copy)
    for d in ORDER:
        other = peer_of(p, d)
        if d == PEERS // 2:
            pl.semaphore_wait(row, 1)
        for part, src in enumerate((k, v)):
            small[d, part] = remote(
                src.at[:, pl.ds(pl.multiple_of(other * WIDTH, WIDTH), WIDTH)],
                kv.at[core, z, part, pl.ds(p * ROWS, ROWS)],
                kv_s.at[d, part],
                kv_r.at[d, part],
                (z * PEERS + other, t),
            )
    wide = HEADS * WIDTH
    for d in ORDER:
        other = peer_of(p, d)
        for part, (src, dst) in enumerate(((q, qg), (do, dog))):
            large.append(
                remote(
                    src.at[:, pl.ds(pl.multiple_of(other * wide, wide), wide)],
                    dst.at[p],
                    q_s.at[d, part],
                    q_r.at[d, part],
                    (z * PEERS + other, t),
                )
            )
    own_large = []
    for part, (src, dst) in enumerate(((q, qg), (do, dog))):
        copy = pltpu.make_async_copy(
            src.at[:, pl.ds(pl.multiple_of(p * wide, wide), wide)], dst.at[p], q_s.at[0, part]
        )
        copy.start()
        own_large.append(copy)

    def piece(part, half, offset):
        return kv.at[core, (z + offset) % RING, part, half_rows(p, half)]

    def forward(step, way, part, half, offset):
        chunk = piece(part, half, offset)
        key = step, way, part, half
        target = beside(z, p, t, way, 2 if step == 3 else 1)
        ring[key] = remote(chunk, chunk, ring_s.at[key], ring_r.at[key], target)

    def share(part, half, offset):
        chunk = piece(part, half, offset)
        key = offset, part, half
        across.append(remote(chunk, chunk, sib_s.at[key], sib_r.at[key], (here, sibling)))

    for half in range(2):
        for part in range(2):
            if half == 0:
                own[part].wait()
            for d in ORDER:
                if d // 4 == half:
                    small[d, part].wait_recv()
            for way in range(2):
                forward(0, way, part, half, 0)
            share(part, half, 0)
    for step in range(1, 5):
        for half in range(2):
            for part in range(2):
                for way in range(2):
                    if step == 4 and way != part:
                        continue
                    offset = RING - step if way == 0 else step
                    ring[step - 1, way, part, half].wait_recv()
                    if step < 3:
                        forward(step, way, part, half, offset)
                    if step == 2 and way == part:
                        forward(3, way, part, half, offset)
                    share(part, half, offset)
    for copy in across:
        copy.wait_recv()
    for copy in large:
        copy.wait()
    for copy in own_large:
        copy.wait()
    for copy in list(small.values()) + list(ring.values()) + across:
        copy.wait_send()


def attention_kernel(
    spans_in, starts_in, q, do, kv, dq, dkv,
    spans, starts, work_tile, work_row, first_work,
    key, value, dkey, dvalue, queries, grads, lows, highs,
    powers, dweights, tops, totals, dots, tile_top, tile_inverse, tile_delta, dq_sum, sems,
):
    loads = [
        pltpu.make_async_copy(spans_in, spans, sems.at[0]),
        pltpu.make_async_copy(starts_in, starts, sems.at[1]),
    ]
    for copy in loads:
        copy.start()
    z, p, t, y_lo, core = place()
    del p, t
    base = y_lo * KEYS

    def clear(b, _):
        rows = pl.ds(pl.multiple_of(b * BLOCK, BLOCK), BLOCK)
        dkey[rows] = jnp.zeros((BLOCK, WIDTH), jnp.float32)
        dvalue[rows] = jnp.zeros((BLOCK, WIDTH), jnp.float32)
        return 0

    lax.fori_loop(0, KEYS // BLOCK + 1, clear, 0)
    value[KEYS:] = jnp.zeros((BLOCK, WIDTH), jnp.bfloat16)
    key[KEYS:] = jnp.zeros((BLOCK, WIDTH), jnp.bfloat16)
    dq_sum[...] = jnp.zeros_like(dq_sum)
    for i in range(PEERS):
        for h in range(HEADS):
            part = slice(h * WIDTH, (h + 1) * WIDTH)
            queries[i, h * ROWS : (h + 1) * ROWS] = q[i, :, part]
            grads[i, h * ROWS : (h + 1) * ROWS] = do[i, :, part]
    for copy in loads:
        copy.wait()

    def local_row(c, half):
        return pl.multiple_of(spans[2 * c + y_lo] * SPAN - base + half * ROWS, ROWS)

    def place_keys(i, _):
        for j in range(PEERS):
            for half in range(2):
                row = local_row(i * PEERS + j, half)
                key[pl.ds(row, ROWS)] = kv[half, i, 0, j * ROWS : (j + 1) * ROWS]
                value[pl.ds(row, ROWS)] = kv[half, i, 1, j * ROWS : (j + 1) * ROWS]
        return 0

    lax.fori_loop(0, RING, place_keys, 0)

    columns = HEADS * ROWS

    def plan(i, count):
        first = local_row(z * PEERS + i, core)
        row = first + lax.broadcasted_iota(jnp.int32, (1, columns), 1) % ROWS
        begin = jnp.int32(0)
        low = jnp.zeros((1, columns), jnp.int32)
        for n in range(starts.shape[0]):
            start = starts[n] - base
            begin = jnp.where(start <= first, jnp.maximum(begin, start), begin)
            low = jnp.where(start <= row, jnp.maximum(low, start), low)
        lows[i] = low
        highs[i] = row
        begin = (begin // WIDTH) * WIDTH
        steps = (first + ROWS - begin + BLOCK - 1) // BLOCK
        first_work[i] = count

        def enter(b, _):
            work_tile[count + b] = i
            work_row[count + b] = begin + b * BLOCK
            return 0

        lax.fori_loop(0, steps, enter, 0)
        return count + steps

    count = lax.fori_loop(0, PEERS, plan, jnp.int32(0))
    first_work[PEERS] = count
    for u in range(TOGETHER - 1):
        work_tile[count + u] = 0
        work_row[count + u] = KEYS
    groups = (count + TOGETHER - 1) // TOGETHER

    def score_group(g, _):
        products = []
        for u in range(TOGETHER):
            n = g * TOGETHER + u
            i = work_tile[n]
            here = pl.multiple_of(work_row[n], WIDTH)
            rows = pl.ds(here, BLOCK)
            s = lax.dot_general(
                key[rows], queries[i], (((1,), (1,)), ((), ())), preferred_element_type=jnp.float32
            )
            dw = lax.dot_general(
                value[rows], grads[i], (((1,), (1,)), ((), ())), preferred_element_type=jnp.float32
            )
            products.append((here, lows[i], highs[i], s, dw))
        for u, (here, low, high, s, dw) in enumerate(products):
            n = g * TOGETHER + u
            pos = here + lax.broadcasted_iota(jnp.int32, (BLOCK, columns), 0)
            s = jnp.where((pos - low).astype(jnp.uint32) <= (high - low).astype(jnp.uint32), s * SCALE_LOG2, NEG_BIG)
            top = jnp.max(s, axis=0, keepdims=True)
            e = jnp.exp2(s - top)
            dweights[n] = dw
            powers[n] = s
            tops[pl.ds(n, 1)] = top
            totals[pl.ds(n, 1)] = jnp.sum(e, axis=0, keepdims=True)
            dots[pl.ds(n, 1)] = jnp.sum(e * dw, axis=0, keepdims=True)
        return 0

    lax.fori_loop(0, groups, score_group, 0)
    entry = lax.broadcasted_iota(jnp.int32, (WORK, 1), 0)
    for i in range(PEERS):
        mine = (entry >= first_work[i]) & (entry < first_work[i + 1])
        tops_i = jnp.where(mine, tops[:WORK], NEG_BIG)
        top = jnp.max(tops_i, axis=0, keepdims=True)
        factor = jnp.exp2(tops_i - top)
        total = jnp.sum(jnp.where(mine, totals[:WORK] * factor, 0.0), axis=0, keepdims=True)
        dot = jnp.sum(jnp.where(mine, dots[:WORK] * factor, 0.0), axis=0, keepdims=True)
        inverse = 1.0 / total
        tile_top[i] = top + jnp.log2(total)
        tile_inverse[i] = inverse
        tile_delta[i] = dot * inverse

    def grad_group(g, _):
        products = []
        for u in range(TOGETHER):
            n = g * TOGETHER + u
            i = work_tile[n]
            rows = pl.ds(pl.multiple_of(work_row[n], WIDTH), BLOCK)
            w = jnp.exp2(powers[n] - tile_top[i])
            ds = (w * (dweights[n] - tile_delta[i])).astype(jnp.bfloat16)
            w = w.astype(jnp.bfloat16)
            products.append(
                (
                    i,
                    rows,
                    jnp.dot(w, grads[i], preferred_element_type=jnp.float32),
                    jnp.dot(ds, queries[i], preferred_element_type=jnp.float32),
                    lax.dot_general(
                        ds, key[rows], (((0,), (0,)), ((), ())), preferred_element_type=jnp.float32
                    ),
                )
            )
        for i, rows, to_value, to_key, to_query in products:
            dvalue[rows] += to_value
            dkey[rows] += to_key
            dq_sum[i] += to_query
        return 0

    lax.fori_loop(0, groups, grad_group, 0)
    for i in range(PEERS):
        out = (dq_sum[i] * SCALE).astype(jnp.bfloat16)
        for h in range(HEADS):
            dq[i, :, h * WIDTH : (h + 1) * WIDTH] = out[h * ROWS : (h + 1) * ROWS]

    def give_keys(i, _):
        for j in range(PEERS):
            for half in range(2):
                rows = pl.ds(local_row(i * PEERS + j, half), ROWS)
                slot = slice(j * ROWS, (j + 1) * ROWS)
                dkv[half, i, 0, slot] = (dkey[rows] * SCALE).astype(jnp.bfloat16)
                dkv[half, i, 1, slot] = dvalue[rows].astype(jnp.bfloat16)
        return 0

    lax.fori_loop(0, RING, give_keys, 0)


def scatter_kernel(
    dqp, dkv, dq, dk, dv, pair, got, sent, final,
    pair_s, pair_r, q_s, q_r, ring_s, ring_r, kv_s, kv_r, row,
):
    z, p, t, y_lo, core = place()
    here = z * PEERS + p
    sibling = y_lo * 2 + 1 - core
    across, large, ring, small = {}, [], {}, []
    greet(z, p, t, sibling, row)
    for offset in (4, 3, 5, 2, 6, 1, 7, 0):
        across[offset] = remote(
            dkv.at[1 - core, (z + offset) % RING],
            pair.at[offset],
            pair_s.at[offset],
            pair_r.at[offset],
            (here, sibling),
        )
    met = set()

    def term(offset, part, half):
        if offset not in met:
            across[offset].wait_recv()
            met.add(offset)
        rows = half_rows(p, half)
        mine = dkv[core, (z + offset) % RING, part, rows].astype(jnp.float32)
        return mine + pair[offset, part, rows].astype(jnp.float32)

    def arrived(step, way, part, half):
        ring[step, way, part, half].wait_recv()
        return got[step, way, part, half_rows(p, half)].astype(jnp.float32)

    def send(step, way, part, half, value):
        rows = half_rows(p, half)
        key = step, way, part, half
        sent[step, way, part, rows] = value.astype(jnp.bfloat16)
        ring[key] = remote(
            sent.at[step, way, part, rows],
            got.at[step, way, part, rows],
            ring_s.at[key],
            ring_r.at[key],
            beside(z, p, t, way, 2 if step == 3 else 1),
        )

    for step in range(3):
        for half in (1, 0):
            if step == 0:
                for way in range(2):
                    send(3, way, way, half, term(4, way, half))
            for part in range(2):
                for way in range(2):
                    value = term(3 - step if way == 0 else RING - 3 + step, part, half)
                    if step > 0:
                        value += arrived(step - 1, way, part, half)
                    if step == 1 and part == way:
                        value += arrived(3, way, part, half)
                    send(step, way, part, half, value)
        if step == 0:
            pl.semaphore_wait(row, 1)
            wide = HEADS * WIDTH
            columns = pl.ds(pl.multiple_of(p * wide, wide), wide)
            for d in ORDER:
                other = peer_of(p, d)
                large.append(
                    remote(
                        dqp.at[other], dq.at[:, columns], q_s.at[d], q_r.at[d], (z * PEERS + other, t)
                    )
                )
            own_large = pltpu.make_async_copy(dqp.at[p], dq.at[:, columns], q_s.at[0])
            own_large.start()
    narrow = pl.ds(pl.multiple_of(p * WIDTH, WIDTH), WIDTH)
    own_small = []
    for half in (1, 0):
        for part, dst in enumerate((dk, dv)):
            value = term(0, part, half)
            for way in range(2):
                value += arrived(2, way, part, half)
            final[part, half_rows(p, half)] = value.astype(jnp.bfloat16)
            for d in range(PEERS):
                if d // 4 != half:
                    continue
                other = peer_of(p, d)
                src = final.at[part, pl.ds(other * ROWS, ROWS)]
                if d == 0:
                    copy = pltpu.make_async_copy(src, dst.at[:, narrow], kv_s.at[0, part])
                    copy.start()
                    own_small.append(copy)
                else:
                    small.append(
                        remote(
                            src,
                            dst.at[:, narrow],
                            kv_s.at[d, part],
                            kv_r.at[d, part],
                            (z * PEERS + other, t),
                        )
                    )
    for copy in large + small:
        copy.wait()
    for copy in [own_large] + own_small:
        copy.wait()
    for copy in list(ring.values()) + list(across.values()):
        copy.wait_send()


def attend(span_map, doc_starts, qg, dog, kv):
    vmem = pl.BlockSpec(memory_space=pltpu.VMEM)
    hbm = pl.BlockSpec(memory_space=pltpu.HBM)
    dma = pltpu.SemaphoreType.DMA
    b16, f32 = jnp.bfloat16, jnp.float32
    columns = HEADS * ROWS
    return pl.pallas_call(
        attention_kernel,
        out_shape=(
            jax.ShapeDtypeStruct(qg.shape, b16),
            jax.ShapeDtypeStruct(kv.shape, b16),
        ),
        in_specs=[hbm, hbm, vmem, vmem, vmem],
        out_specs=(vmem, vmem),
        scratch_shapes=[
            pltpu.SMEM(span_map.shape, jnp.int32),
            pltpu.SMEM(doc_starts.shape, jnp.int32),
            pltpu.SMEM((WORK + TOGETHER,), jnp.int32),
            pltpu.SMEM((WORK + TOGETHER,), jnp.int32),
            pltpu.SMEM((PEERS + 1,), jnp.int32),
            pltpu.VMEM((KEYS + BLOCK, WIDTH), b16),
            pltpu.VMEM((KEYS + BLOCK, WIDTH), b16),
            pltpu.VMEM((KEYS + BLOCK, WIDTH), f32),
            pltpu.VMEM((KEYS + BLOCK, WIDTH), f32),
            pltpu.VMEM((PEERS, columns, WIDTH), b16),
            pltpu.VMEM((PEERS, columns, WIDTH), b16),
            pltpu.VMEM((PEERS, 1, columns), jnp.int32),
            pltpu.VMEM((PEERS, 1, columns), jnp.int32),
            pltpu.VMEM((WORK + TOGETHER, BLOCK, columns), f32),
            pltpu.VMEM((WORK + TOGETHER, BLOCK, columns), f32),
            pltpu.VMEM((WORK + 8, columns), f32),
            pltpu.VMEM((WORK + 8, columns), f32),
            pltpu.VMEM((WORK + 8, columns), f32),
            pltpu.VMEM((PEERS, 1, columns), f32),
            pltpu.VMEM((PEERS, 1, columns), f32),
            pltpu.VMEM((PEERS, 1, columns), f32),
            pltpu.VMEM((PEERS, columns, WIDTH), f32),
            dma((2,)),
        ],
        compiler_params=pltpu.CompilerParams(vmem_limit_bytes=48 * 1024 * 1024),
        name="attention_grads",
    )(span_map, doc_starts, qg, dog, kv)


def gather(queries, output_gradient, key_head_states, value_head_states):
    anywhere = pl.BlockSpec(memory_space=pl.ANY)
    vmem = pl.BlockSpec(memory_space=pltpu.VMEM)
    hbm = pl.BlockSpec(memory_space=pltpu.HBM)
    dma = pltpu.SemaphoreType.DMA
    b16 = jnp.bfloat16
    wide = HEADS * WIDTH
    rows = PEERS * ROWS
    grouped = jax.ShapeDtypeStruct((PEERS, ROWS, wide), b16)
    chunks = jax.ShapeDtypeStruct((2, RING, 2, rows, WIDTH), b16)
    return pl.pallas_call(
        gather_kernel,
        out_shape=(grouped, grouped, chunks),
        in_specs=[hbm] * 4,
        out_specs=(anywhere,) * 3,
        scratch_shapes=[
            dma((PEERS, 2)),
            dma((PEERS, 2)),
            dma((PEERS, 2)),
            dma((PEERS, 2)),
            dma((4, 2, 2, 2)),
            dma((4, 2, 2, 2)),
            dma((RING, 2, 2)),
            dma((RING, 2, 2)),
            pltpu.SemaphoreType.REGULAR,
        ],
        compiler_params=pltpu.CompilerParams(
            collective_id=0, has_side_effects=True, vmem_limit_bytes=2 * 1024 * 1024
        ),
        name="gather_heads",
    )(queries, output_gradient, key_head_states, value_head_states)


def scatter(dqp, dkv):
    anywhere = pl.BlockSpec(memory_space=pl.ANY)
    vmem = pl.BlockSpec(memory_space=pltpu.VMEM)
    hbm = pl.BlockSpec(memory_space=pltpu.HBM)
    dma = pltpu.SemaphoreType.DMA
    b16 = jnp.bfloat16
    wide = HEADS * WIDTH
    rows = PEERS * ROWS
    return pl.pallas_call(
        scatter_kernel,
        out_shape=(
            jax.ShapeDtypeStruct((ROWS, PEERS * wide), b16),
            jax.ShapeDtypeStruct((ROWS, PEERS * WIDTH), b16),
            jax.ShapeDtypeStruct((ROWS, PEERS * WIDTH), b16),
        ),
        in_specs=[anywhere, vmem],
        out_specs=(anywhere,) * 3,
        scratch_shapes=[
            pltpu.VMEM((RING, 2, rows, WIDTH), b16),
            pltpu.VMEM((4, 2, 2, rows, WIDTH), b16),
            pltpu.VMEM((4, 2, 2, rows, WIDTH), b16),
            pltpu.VMEM((2, rows, WIDTH), b16),
            dma((RING,)),
            dma((RING,)),
            dma((PEERS,)),
            dma((PEERS,)),
            dma((4, 2, 2, 2)),
            dma((4, 2, 2, 2)),
            dma((PEERS, 2)),
            dma((PEERS, 2)),
            pltpu.SemaphoreType.REGULAR,
        ],
        compiler_params=pltpu.CompilerParams(
            collective_id=1, has_side_effects=True, vmem_limit_bytes=12 * 1024 * 1024
        ),
        name="scatter_grads",
    )(dqp, dkv)


def finish_kernel(dq_in, dk_in, dv_in, dq, dk, dv, sems):
    copies = [
        pltpu.make_async_copy(src, dst, sems.at[n])
        for n, (src, dst) in enumerate(((dq_in, dq), (dk_in, dk), (dv_in, dv)))
    ]
    for copy in copies:
        copy.start()
    for copy in copies:
        copy.wait()


def finish(*grads):
    anywhere = pl.BlockSpec(memory_space=pl.ANY)
    hbm = pl.BlockSpec(memory_space=pltpu.HBM)
    return pl.pallas_call(
        finish_kernel,
        out_shape=tuple(jax.ShapeDtypeStruct(x.shape, x.dtype) for x in grads),
        in_specs=[anywhere] * 3,
        out_specs=(hbm,) * 3,
        scratch_shapes=[pltpu.SemaphoreType.DMA((3,))],
        compiler_params=pltpu.CompilerParams(vmem_limit_bytes=1024 * 1024),
        name="finish",
    )(*grads)


def shards(queries, key_head_states, value_head_states, output_gradient, doc_starts, span_map):
    queries, output_gradient, key_head_states, value_head_states, span_map, doc_starts = (
        pltpu.with_memory_space_constraint(x, pltpu.HBM)
        for x in (queries, output_gradient, key_head_states, value_head_states, span_map, doc_starts)
    )
    qg, dog, kv = gather(queries, output_gradient, key_head_states, value_head_states)
    dqp, dkv = attend(span_map, doc_starts, qg, dog, kv)
    return finish(*scatter(dqp, dkv))


def solution(mesh):
    rows = P(("ctx", "tp"), None)
    in_specs = (rows, rows, rows, rows, P(), P())
    return jax.shard_map(
        shards, mesh=mesh, in_specs=in_specs, out_specs=(rows, rows, rows), check_vma=False
    )
```

```python
import math

import jax
import jax.numpy as jnp
from jax import lax
from jax.experimental import pallas as pl
from jax.experimental.pallas import tpu as pltpu
from jax.sharding import PartitionSpec as P

MESH = pl.DeviceIdType.MESH
ORDER = (1, 3, 2, 4, 5, 7, 6)
HEADS = 8
WIDTH = 128
ROWS = 32
PEERS = 8
RING = 8
SPAN = 64
KEYS = 4096
BLOCK = 256
CLEAR = 64
TOGETHER = 7
WORK = PEERS * -(-2048 // BLOCK)
SCALE = 1.0 / math.sqrt(WIDTH)
SCALE_LOG2 = SCALE * math.log2(math.e)
NEG_BIG = -1e30


def place():
    c, t = lax.axis_index("ctx"), lax.axis_index("tp")
    return c // PEERS, c % PEERS, t, t // 2, t % 2


def peer_of(p, d):
    return ((p // 4 + d // 4) % 2) * 4 + (p % 4 + d % 4) % 4


def half_rows(p, half):
    rows = PEERS * ROWS // 2
    return pl.ds(pl.multiple_of(((p // 4 + half) % 2) * rows, rows), rows)


def beside(z, p, t, way, far):
    return along_z(z, p, far if way == 0 else RING - far), t


def along_z(z, p, offset):
    return ((z + offset) % RING) * PEERS + p


def greet(z, p, t, sibling, row):
    barrier = pltpu.get_barrier_semaphore()
    targets = [(z * PEERS + peer_of(p, d), t) for d in range(1, PEERS // 2 + 1)]
    targets += [(along_z(z, p, offset), t) for offset in (1, 2, RING - 2, RING - 1)]
    targets.append((z * PEERS + p, sibling))
    for target in targets:
        pl.semaphore_signal(barrier, inc=1, device_id=target, device_id_type=MESH)
    pl.semaphore_wait(barrier, len(targets))
    across = (z * PEERS + peer_of(p, PEERS // 2), t)
    pl.semaphore_signal(row, inc=1, device_id=across, device_id_type=MESH)


def remote(src, dst, send, recv, target):
    copy = pltpu.make_async_remote_copy(
        src_ref=src, dst_ref=dst, send_sem=send, recv_sem=recv, device_id=target, device_id_type=MESH
    )
    copy.start()
    return copy


def gather_kernel(
    q, do, k, v, qg, dog, kv, kv_s, kv_r, q_s, q_r, ring_s, ring_r, sib_s, sib_r, row
):
    z, p, t, y_lo, core = place()
    here = z * PEERS + p
    sibling = y_lo * 2 + 1 - core
    greet(z, p, t, sibling, row)
    small, large, ring, across, own = {}, [], {}, [], []
    for part, src in enumerate((k, v)):
        copy = pltpu.make_async_copy(
            src.at[:, pl.ds(pl.multiple_of(p * WIDTH, WIDTH), WIDTH)],
            kv.at[core, z, part, pl.ds(p * ROWS, ROWS)],
            kv_s.at[0, part],
        )
        copy.start()
        own.append(copy)
    for d in ORDER:
        other = peer_of(p, d)
        if d == PEERS // 2:
            pl.semaphore_wait(row, 1)
        for part, src in enumerate((k, v)):
            small[d, part] = remote(
                src.at[:, pl.ds(pl.multiple_of(other * WIDTH, WIDTH), WIDTH)],
                kv.at[core, z, part, pl.ds(p * ROWS, ROWS)],
                kv_s.at[d, part],
                kv_r.at[d, part],
                (z * PEERS + other, t),
            )
    wide = HEADS * WIDTH
    for d in ORDER:
        other = peer_of(p, d)
        for part, (src, dst) in enumerate(((q, qg), (do, dog))):
            large.append(
                remote(
                    src.at[:, pl.ds(pl.multiple_of(other * wide, wide), wide)],
                    dst.at[p],
                    q_s.at[d, part],
                    q_r.at[d, part],
                    (z * PEERS + other, t),
                )
            )
    own_large = []
    for part, (src, dst) in enumerate(((q, qg), (do, dog))):
        copy = pltpu.make_async_copy(
            src.at[:, pl.ds(pl.multiple_of(p * wide, wide), wide)], dst.at[p], q_s.at[0, part]
        )
        copy.start()
        own_large.append(copy)

    def piece(part, half, offset):
        return kv.at[core, (z + offset) % RING, part, half_rows(p, half)]

    def forward(step, way, part, half, offset):
        chunk = piece(part, half, offset)
        key = step, way, part, half
        target = beside(z, p, t, way, 2 if step == 3 else 1)
        ring[key] = remote(chunk, chunk, ring_s.at[key], ring_r.at[key], target)

    def share(part, half, offset):
        chunk = piece(part, half, offset)
        key = offset, part, half
        across.append(remote(chunk, chunk, sib_s.at[key], sib_r.at[key], (here, sibling)))

    for half in range(2):
        for part in range(2):
            if half == 0:
                own[part].wait()
            for d in ORDER:
                if d // 4 == half:
                    small[d, part].wait_recv()
            for way in range(2):
                forward(0, way, part, half, 0)
            share(part, half, 0)
    for step in range(1, 5):
        for half in range(2):
            for part in range(2):
                for way in range(2):
                    if step == 4 and way != part:
                        continue
                    offset = RING - step if way == 0 else step
                    ring[step - 1, way, part, half].wait_recv()
                    if step < 3:
                        forward(step, way, part, half, offset)
                    if step == 2 and way == part:
                        forward(3, way, part, half, offset)
                    share(part, half, offset)
    for copy in across:
        copy.wait_recv()
    for copy in large:
        copy.wait()
    for copy in own_large:
        copy.wait()
    for copy in list(small.values()) + list(ring.values()) + across:
        copy.wait_send()


def attention_kernel(
    spans_in, starts_in, q, do, kv, dq, dkv,
    spans, starts, work_tile, work_row, first_work,
    key, value, dkey, dvalue, queries, grads, lows, highs,
    powers, dweights, tops, totals, dots, tile_top, tile_inverse, tile_delta, dq_sum, sems,
):
    loads = [
        pltpu.make_async_copy(spans_in, spans, sems.at[0]),
        pltpu.make_async_copy(starts_in, starts, sems.at[1]),
    ]
    for copy in loads:
        copy.start()
    z, p, t, y_lo, core = place()
    del p, t
    base = y_lo * KEYS

    def clear(b, _):
        rows = pl.ds(pl.multiple_of(b * CLEAR, CLEAR), CLEAR)
        dkey[rows] = jnp.zeros((CLEAR, WIDTH), jnp.float32)
        dvalue[rows] = jnp.zeros((CLEAR, WIDTH), jnp.float32)
        return 0

    lax.fori_loop(0, (KEYS + BLOCK) // CLEAR, clear, 0)
    value[KEYS:] = jnp.zeros((BLOCK, WIDTH), jnp.bfloat16)
    key[KEYS:] = jnp.zeros((BLOCK, WIDTH), jnp.bfloat16)
    dq_sum[...] = jnp.zeros_like(dq_sum)
    for i in range(PEERS):
        for h in range(HEADS):
            part = slice(h * WIDTH, (h + 1) * WIDTH)
            queries[i, h * ROWS : (h + 1) * ROWS] = q[i, :, part]
            grads[i, h * ROWS : (h + 1) * ROWS] = do[i, :, part]
    for copy in loads:
        copy.wait()

    def local_row(c, half):
        return pl.multiple_of(spans[2 * c + y_lo] * SPAN - base + half * ROWS, ROWS)

    def place_keys(i, _):
        for j in range(PEERS):
            for half in range(2):
                row = local_row(i * PEERS + j, half)
                key[pl.ds(row, ROWS)] = kv[half, i, 0, j * ROWS : (j + 1) * ROWS]
                value[pl.ds(row, ROWS)] = kv[half, i, 1, j * ROWS : (j + 1) * ROWS]
        return 0

    lax.fori_loop(0, RING, place_keys, 0)

    columns = HEADS * ROWS

    def plan(i, count):
        first = local_row(z * PEERS + i, core)
        row = first + lax.broadcasted_iota(jnp.int32, (1, columns), 1) % ROWS
        begin = jnp.int32(0)
        low = jnp.zeros((1, columns), jnp.int32)
        for n in range(starts.shape[0]):
            start = starts[n] - base
            begin = jnp.where(start <= first, jnp.maximum(begin, start), begin)
            low = jnp.where(start <= row, jnp.maximum(low, start), low)
        lows[i] = low
        highs[i] = row
        begin = (begin // ROWS) * ROWS
        steps = (first + ROWS - begin + BLOCK - 1) // BLOCK
        first_work[i] = count

        def enter(b, _):
            work_tile[count + b] = i
            work_row[count + b] = begin + b * BLOCK
            return 0

        lax.fori_loop(0, steps, enter, 0)
        return count + steps

    count = jnp.int32(0)
    for i in range(PEERS):
        count = plan(i, count)
    first_work[PEERS] = count
    for u in range(TOGETHER - 1):
        work_tile[count + u] = 0
        work_row[count + u] = KEYS
    groups = (count + TOGETHER - 1) // TOGETHER

    def score_group(g, _):
        products = []
        for u in range(TOGETHER):
            n = g * TOGETHER + u
            i = work_tile[n]
            here = pl.multiple_of(work_row[n], ROWS)
            rows = pl.ds(here, BLOCK)
            s = lax.dot_general(
                key[rows], queries[i], (((1,), (1,)), ((), ())), preferred_element_type=jnp.float32
            )
            dw = lax.dot_general(
                value[rows], grads[i], (((1,), (1,)), ((), ())), preferred_element_type=jnp.float32
            )
            products.append((here, lows[i], highs[i], s, dw))
        for u, (here, low, high, s, dw) in enumerate(products):
            n = g * TOGETHER + u
            pos = here + lax.broadcasted_iota(jnp.int32, (BLOCK, columns), 0)
            s = jnp.where((pos - low).astype(jnp.uint32) <= (high - low).astype(jnp.uint32), s * SCALE_LOG2, NEG_BIG)
            top = jnp.max(s, axis=0, keepdims=True)
            e = jnp.exp2(s - top)
            dweights[n] = dw
            powers[n] = s
            tops[pl.ds(n, 1)] = top
            totals[pl.ds(n, 1)] = jnp.sum(e, axis=0, keepdims=True)
            dots[pl.ds(n, 1)] = jnp.sum(e * dw, axis=0, keepdims=True)
        return 0

    lax.fori_loop(0, groups, score_group, 0)
    entry = lax.broadcasted_iota(jnp.int32, (WORK, 1), 0)
    for i in range(PEERS):
        mine = (entry >= first_work[i]) & (entry < first_work[i + 1])
        tops_i = jnp.where(mine, tops[:WORK], NEG_BIG)
        top = jnp.max(tops_i, axis=0, keepdims=True)
        factor = jnp.exp2(tops_i - top)
        total = jnp.sum(jnp.where(mine, totals[:WORK] * factor, 0.0), axis=0, keepdims=True)
        dot = jnp.sum(jnp.where(mine, dots[:WORK] * factor, 0.0), axis=0, keepdims=True)
        inverse = 1.0 / total
        tile_top[i] = top + jnp.log2(total)
        tile_inverse[i] = inverse
        tile_delta[i] = dot * inverse

    def grad_group(g, _):
        products = []
        for u in range(TOGETHER):
            n = g * TOGETHER + u
            i = work_tile[n]
            rows = pl.ds(pl.multiple_of(work_row[n], ROWS), BLOCK)
            w = jnp.exp2(powers[n] - tile_top[i])
            ds = (w * (dweights[n] - tile_delta[i])).astype(jnp.bfloat16)
            w = w.astype(jnp.bfloat16)
            products.append(
                (
                    i,
                    rows,
                    jnp.dot(w, grads[i], preferred_element_type=jnp.float32),
                    jnp.dot(ds, queries[i], preferred_element_type=jnp.float32),
                    lax.dot_general(
                        ds, key[rows], (((0,), (0,)), ((), ())), preferred_element_type=jnp.float32
                    ),
                )
            )
        for i, rows, to_value, to_key, to_query in products:
            dvalue[rows] += to_value
            dkey[rows] += to_key
            dq_sum[i] += to_query
        return 0

    lax.fori_loop(0, groups, grad_group, 0)
    for i in range(PEERS):
        out = (dq_sum[i] * SCALE).astype(jnp.bfloat16)
        for h in range(HEADS):
            dq[i, :, h * WIDTH : (h + 1) * WIDTH] = out[h * ROWS : (h + 1) * ROWS]

    def give_keys(i, _):
        for j in range(PEERS):
            for half in range(2):
                rows = pl.ds(local_row(i * PEERS + j, half), ROWS)
                slot = slice(j * ROWS, (j + 1) * ROWS)
                dkv[half, i, 0, slot] = (dkey[rows] * SCALE).astype(jnp.bfloat16)
                dkv[half, i, 1, slot] = dvalue[rows].astype(jnp.bfloat16)
        return 0

    lax.fori_loop(0, RING, give_keys, 0)


def scatter_kernel(
    dqp, dkv, dq, dk, dv, pair, got, sent, final,
    pair_s, pair_r, q_s, q_r, ring_s, ring_r, kv_s, kv_r, row,
):
    z, p, t, y_lo, core = place()
    here = z * PEERS + p
    sibling = y_lo * 2 + 1 - core
    across, large, ring, small = {}, [], {}, []
    greet(z, p, t, sibling, row)
    for offset in (4, 3, 5, 2, 6, 1, 7, 0):
        across[offset] = remote(
            dkv.at[1 - core, (z + offset) % RING],
            pair.at[offset],
            pair_s.at[offset],
            pair_r.at[offset],
            (here, sibling),
        )
    met = set()

    def term(offset, part, half):
        if offset not in met:
            across[offset].wait_recv()
            met.add(offset)
        rows = half_rows(p, half)
        mine = dkv[core, (z + offset) % RING, part, rows].astype(jnp.float32)
        return mine + pair[offset, part, rows].astype(jnp.float32)

    def arrived(step, way, part, half):
        ring[step, way, part, half].wait_recv()
        return got[step, way, part, half_rows(p, half)].astype(jnp.float32)

    def send(step, way, part, half, value):
        rows = half_rows(p, half)
        key = step, way, part, half
        sent[step, way, part, rows] = value.astype(jnp.bfloat16)
        ring[key] = remote(
            sent.at[step, way, part, rows],
            got.at[step, way, part, rows],
            ring_s.at[key],
            ring_r.at[key],
            beside(z, p, t, way, 2 if step == 3 else 1),
        )

    for step in range(3):
        for half in (1, 0):
            if step == 0:
                for way in range(2):
                    send(3, way, way, half, term(4, way, half))
            for part in range(2):
                for way in range(2):
                    value = term(3 - step if way == 0 else RING - 3 + step, part, half)
                    if step > 0:
                        value += arrived(step - 1, way, part, half)
                    if step == 1 and part == way:
                        value += arrived(3, way, part, half)
                    send(step, way, part, half, value)
        if step == 0:
            pl.semaphore_wait(row, 1)
            wide = HEADS * WIDTH
            columns = pl.ds(pl.multiple_of(p * wide, wide), wide)
            for d in ORDER:
                other = peer_of(p, d)
                large.append(
                    remote(
                        dqp.at[other], dq.at[:, columns], q_s.at[d], q_r.at[d], (z * PEERS + other, t)
                    )
                )
            own_large = pltpu.make_async_copy(dqp.at[p], dq.at[:, columns], q_s.at[0])
            own_large.start()
    narrow = pl.ds(pl.multiple_of(p * WIDTH, WIDTH), WIDTH)
    own_small = []
    for half in (1, 0):
        for part, dst in enumerate((dk, dv)):
            value = term(0, part, half)
            for way in range(2):
                value += arrived(2, way, part, half)
            final[part, half_rows(p, half)] = value.astype(jnp.bfloat16)
            for d in range(PEERS):
                if d // 4 != half:
                    continue
                other = peer_of(p, d)
                src = final.at[part, pl.ds(other * ROWS, ROWS)]
                if d == 0:
                    copy = pltpu.make_async_copy(src, dst.at[:, narrow], kv_s.at[0, part])
                    copy.start()
                    own_small.append(copy)
                else:
                    small.append(
                        remote(
                            src,
                            dst.at[:, narrow],
                            kv_s.at[d, part],
                            kv_r.at[d, part],
                            (z * PEERS + other, t),
                        )
                    )
    for copy in large + small:
        copy.wait()
    for copy in [own_large] + own_small:
        copy.wait()
    for copy in list(ring.values()) + list(across.values()):
        copy.wait_send()


def attend(span_map, doc_starts, qg, dog, kv):
    vmem = pl.BlockSpec(memory_space=pltpu.VMEM)
    hbm = pl.BlockSpec(memory_space=pltpu.HBM)
    dma = pltpu.SemaphoreType.DMA
    b16, f32 = jnp.bfloat16, jnp.float32
    columns = HEADS * ROWS
    return pl.pallas_call(
        attention_kernel,
        out_shape=(
            jax.ShapeDtypeStruct(qg.shape, b16),
            jax.ShapeDtypeStruct(kv.shape, b16),
        ),
        in_specs=[hbm, hbm, vmem, vmem, vmem],
        out_specs=(vmem, vmem),
        scratch_shapes=[
            pltpu.SMEM(span_map.shape, jnp.int32),
            pltpu.SMEM(doc_starts.shape, jnp.int32),
            pltpu.SMEM((WORK + TOGETHER,), jnp.int32),
            pltpu.SMEM((WORK + TOGETHER,), jnp.int32),
            pltpu.SMEM((PEERS + 1,), jnp.int32),
            pltpu.VMEM((KEYS + BLOCK, WIDTH), b16),
            pltpu.VMEM((KEYS + BLOCK, WIDTH), b16),
            pltpu.VMEM((KEYS + BLOCK, WIDTH), f32),
            pltpu.VMEM((KEYS + BLOCK, WIDTH), f32),
            pltpu.VMEM((PEERS, columns, WIDTH), b16),
            pltpu.VMEM((PEERS, columns, WIDTH), b16),
            pltpu.VMEM((PEERS, 1, columns), jnp.int32),
            pltpu.VMEM((PEERS, 1, columns), jnp.int32),
            pltpu.VMEM((WORK + TOGETHER, BLOCK, columns), f32),
            pltpu.VMEM((WORK + TOGETHER, BLOCK, columns), f32),
            pltpu.VMEM((WORK + 8 + TOGETHER, columns), f32),
            pltpu.VMEM((WORK + 8 + TOGETHER, columns), f32),
            pltpu.VMEM((WORK + 8 + TOGETHER, columns), f32),
            pltpu.VMEM((PEERS, 1, columns), f32),
            pltpu.VMEM((PEERS, 1, columns), f32),
            pltpu.VMEM((PEERS, 1, columns), f32),
            pltpu.VMEM((PEERS, columns, WIDTH), f32),
            dma((2,)),
        ],
        compiler_params=pltpu.CompilerParams(vmem_limit_bytes=48 * 1024 * 1024),
        name="attention_grads",
    )(span_map, doc_starts, qg, dog, kv)


def gather(queries, output_gradient, key_head_states, value_head_states):
    anywhere = pl.BlockSpec(memory_space=pl.ANY)
    vmem = pl.BlockSpec(memory_space=pltpu.VMEM)
    hbm = pl.BlockSpec(memory_space=pltpu.HBM)
    dma = pltpu.SemaphoreType.DMA
    b16 = jnp.bfloat16
    wide = HEADS * WIDTH
    rows = PEERS * ROWS
    grouped = jax.ShapeDtypeStruct((PEERS, ROWS, wide), b16)
    chunks = jax.ShapeDtypeStruct((2, RING, 2, rows, WIDTH), b16)
    return pl.pallas_call(
        gather_kernel,
        out_shape=(grouped, grouped, chunks),
        in_specs=[hbm] * 4,
        out_specs=(anywhere,) * 3,
        scratch_shapes=[
            dma((PEERS, 2)),
            dma((PEERS, 2)),
            dma((PEERS, 2)),
            dma((PEERS, 2)),
            dma((4, 2, 2, 2)),
            dma((4, 2, 2, 2)),
            dma((RING, 2, 2)),
            dma((RING, 2, 2)),
            pltpu.SemaphoreType.REGULAR,
        ],
        compiler_params=pltpu.CompilerParams(
            collective_id=0, has_side_effects=True, vmem_limit_bytes=2 * 1024 * 1024
        ),
        name="gather_heads",
    )(queries, output_gradient, key_head_states, value_head_states)


def scatter(dqp, dkv):
    anywhere = pl.BlockSpec(memory_space=pl.ANY)
    vmem = pl.BlockSpec(memory_space=pltpu.VMEM)
    hbm = pl.BlockSpec(memory_space=pltpu.HBM)
    dma = pltpu.SemaphoreType.DMA
    b16 = jnp.bfloat16
    wide = HEADS * WIDTH
    rows = PEERS * ROWS
    return pl.pallas_call(
        scatter_kernel,
        out_shape=(
            jax.ShapeDtypeStruct((ROWS, PEERS * wide), b16),
            jax.ShapeDtypeStruct((ROWS, PEERS * WIDTH), b16),
            jax.ShapeDtypeStruct((ROWS, PEERS * WIDTH), b16),
        ),
        in_specs=[anywhere, vmem],
        out_specs=(anywhere,) * 3,
        scratch_shapes=[
            pltpu.VMEM((RING, 2, rows, WIDTH), b16),
            pltpu.VMEM((4, 2, 2, rows, WIDTH), b16),
            pltpu.VMEM((4, 2, 2, rows, WIDTH), b16),
            pltpu.VMEM((2, rows, WIDTH), b16),
            dma((RING,)),
            dma((RING,)),
            dma((PEERS,)),
            dma((PEERS,)),
            dma((4, 2, 2, 2)),
            dma((4, 2, 2, 2)),
            dma((PEERS, 2)),
            dma((PEERS, 2)),
            pltpu.SemaphoreType.REGULAR,
        ],
        compiler_params=pltpu.CompilerParams(
            collective_id=1, has_side_effects=True, vmem_limit_bytes=12 * 1024 * 1024
        ),
        name="scatter_grads",
    )(dqp, dkv)


def finish_kernel(dq_in, dk_in, dv_in, dq, dk, dv, sems):
    copies = [
        pltpu.make_async_copy(src, dst, sems.at[n])
        for n, (src, dst) in enumerate(((dq_in, dq), (dk_in, dk), (dv_in, dv)))
    ]
    for copy in copies:
        copy.start()
    for copy in copies:
        copy.wait()


def finish(*grads):
    anywhere = pl.BlockSpec(memory_space=pl.ANY)
    hbm = pl.BlockSpec(memory_space=pltpu.HBM)
    return pl.pallas_call(
        finish_kernel,
        out_shape=tuple(jax.ShapeDtypeStruct(x.shape, x.dtype) for x in grads),
        in_specs=[anywhere] * 3,
        out_specs=(hbm,) * 3,
        scratch_shapes=[pltpu.SemaphoreType.DMA((3,))],
        compiler_params=pltpu.CompilerParams(vmem_limit_bytes=1024 * 1024),
        name="finish",
    )(*grads)


def shards(queries, key_head_states, value_head_states, output_gradient, doc_starts, span_map):
    queries, output_gradient, key_head_states, value_head_states, span_map, doc_starts = (
        pltpu.with_memory_space_constraint(x, pltpu.HBM)
        for x in (queries, output_gradient, key_head_states, value_head_states, span_map, doc_starts)
    )
    qg, dog, kv = gather(queries, output_gradient, key_head_states, value_head_states)
    dqp, dkv = attend(span_map, doc_starts, qg, dog, kv)
    return finish(*scatter(dqp, dkv))


def solution(mesh):
    rows = P(("ctx", "tp"), None)
    in_specs = (rows, rows, rows, rows, P(), P())
    return jax.shard_map(
        shards, mesh=mesh, in_specs=in_specs, out_specs=(rows, rows, rows), check_vma=False
    )
```

```python
import math

import jax
import jax.numpy as jnp
from jax import lax
from jax.experimental import pallas as pl
from jax.experimental.pallas import tpu as pltpu
from jax.sharding import PartitionSpec as P

MESH = pl.DeviceIdType.MESH
ORDER = (1, 3, 2, 4, 5, 7, 6)
HEADS = 8
WIDTH = 128
ROWS = 32
PEERS = 8
RING = 8
SPAN = 64
KEYS = 4096
BLOCK = 256
CLEAR = 64
TOGETHER = 7
WORK = PEERS * -(-2048 // BLOCK)
SCALE = 1.0 / math.sqrt(WIDTH)
SCALE_LOG2 = SCALE * math.log2(math.e)
NEG_BIG = -1e30


def place():
    c, t = lax.axis_index("ctx"), lax.axis_index("tp")
    return c // PEERS, c % PEERS, t, t // 2, t % 2


def peer_of(p, d):
    return ((p // 4 + d // 4) % 2) * 4 + (p % 4 + d % 4) % 4


def half_rows(p, half):
    rows = PEERS * ROWS // 2
    return pl.ds(pl.multiple_of(((p // 4 + half) % 2) * rows, rows), rows)


def beside(z, p, t, way, far):
    return along_z(z, p, far if way == 0 else RING - far), t


def along_z(z, p, offset):
    return ((z + offset) % RING) * PEERS + p


def greet(z, p, t, sibling, row):
    barrier = pltpu.get_barrier_semaphore()
    targets = [(z * PEERS + peer_of(p, d), t) for d in range(1, PEERS // 2 + 1)]
    targets += [(along_z(z, p, offset), t) for offset in (1, 2, RING - 2, RING - 1)]
    targets.append((z * PEERS + p, sibling))
    for target in targets:
        pl.semaphore_signal(barrier, inc=1, device_id=target, device_id_type=MESH)
    pl.semaphore_wait(barrier, len(targets))
    across = (z * PEERS + peer_of(p, PEERS // 2), t)
    pl.semaphore_signal(row, inc=1, device_id=across, device_id_type=MESH)


def remote(src, dst, send, recv, target):
    copy = pltpu.make_async_remote_copy(
        src_ref=src, dst_ref=dst, send_sem=send, recv_sem=recv, device_id=target, device_id_type=MESH
    )
    copy.start()
    return copy


def gather_kernel(
    q, do, k, v, qg, dog, kv, kv_s, kv_r, q_s, q_r, ring_s, ring_r, sib_s, sib_r, row
):
    z, p, t, y_lo, core = place()
    here = z * PEERS + p
    sibling = y_lo * 2 + 1 - core
    greet(z, p, t, sibling, row)
    small, large, own_large, ring, across, own = {}, [], [], {}, [], []
    for part, src in enumerate((k, v)):
        copy = pltpu.make_async_copy(
            src.at[:, pl.ds(pl.multiple_of(p * WIDTH, WIDTH), WIDTH)],
            kv.at[core, z, part, pl.ds(p * ROWS, ROWS)],
            kv_s.at[0, part],
        )
        copy.start()
        own.append(copy)
    for d in ORDER:
        other = peer_of(p, d)
        if d == PEERS // 2:
            pl.semaphore_wait(row, 1)
        for part, src in enumerate((k, v)):
            small[d, part] = remote(
                src.at[:, pl.ds(pl.multiple_of(other * WIDTH, WIDTH), WIDTH)],
                kv.at[core, z, part, pl.ds(p * ROWS, ROWS)],
                kv_s.at[d, part],
                kv_r.at[d, part],
                (z * PEERS + other, t),
            )
    def piece(part, half, offset):
        return kv.at[core, (z + offset) % RING, part, half_rows(p, half)]

    def forward(step, way, part, half, offset):
        chunk = piece(part, half, offset)
        key = step, way, part, half
        target = beside(z, p, t, way, 2 if step == 3 else 1)
        ring[key] = remote(chunk, chunk, ring_s.at[key], ring_r.at[key], target)

    def share(part, half, offset):
        chunk = piece(part, half, offset)
        key = offset, part, half
        across.append(remote(chunk, chunk, sib_s.at[key], sib_r.at[key], (here, sibling)))

    def send_rows():
        wide = HEADS * WIDTH
        for d in ORDER:
            other = peer_of(p, d)
            for part, (src, dst) in enumerate(((q, qg), (do, dog))):
                large.append(
                    remote(
                        src.at[:, pl.ds(pl.multiple_of(other * wide, wide), wide)],
                        dst.at[p],
                        q_s.at[d, part],
                        q_r.at[d, part],
                        (z * PEERS + other, t),
                    )
                )
        for part, (src, dst) in enumerate(((q, qg), (do, dog))):
            copy = pltpu.make_async_copy(
                src.at[:, pl.ds(pl.multiple_of(p * wide, wide), wide)], dst.at[p], q_s.at[0, part]
            )
            copy.start()
            own_large.append(copy)

    for half in range(2):
        for part in range(2):
            if half == 0:
                own[part].wait()
            for d in ORDER:
                if d // 4 == half:
                    small[d, part].wait_recv()
            for way in range(2):
                forward(0, way, part, half, 0)
            share(part, half, 0)
        if half == 0:
            send_rows()
    for step in range(1, 5):
        for half in range(2):
            for part in range(2):
                for way in range(2):
                    if step == 4 and way != part:
                        continue
                    offset = RING - step if way == 0 else step
                    ring[step - 1, way, part, half].wait_recv()
                    if step < 3:
                        forward(step, way, part, half, offset)
                    if step == 2 and way == part:
                        forward(3, way, part, half, offset)
                    share(part, half, offset)
    for copy in across:
        copy.wait_recv()
    for copy in large:
        copy.wait()
    for copy in own_large:
        copy.wait()
    for copy in list(small.values()) + list(ring.values()) + across:
        copy.wait_send()


def attention_kernel(
    spans_in, starts_in, q, do, kv, dq, dkv,
    spans, starts, work_tile, work_row, first_work,
    key, value, dkey, dvalue, queries, grads, lows, highs,
    powers, dweights, tops, totals, dots, tile_top, tile_inverse, tile_delta, dq_sum, sems,
):
    loads = [
        pltpu.make_async_copy(spans_in, spans, sems.at[0]),
        pltpu.make_async_copy(starts_in, starts, sems.at[1]),
    ]
    for copy in loads:
        copy.start()
    z, p, t, y_lo, core = place()
    del p, t
    base = y_lo * KEYS

    def clear(b, _):
        rows = pl.ds(pl.multiple_of(b * CLEAR, CLEAR), CLEAR)
        dkey[rows] = jnp.zeros((CLEAR, WIDTH), jnp.float32)
        dvalue[rows] = jnp.zeros((CLEAR, WIDTH), jnp.float32)
        return 0

    lax.fori_loop(0, (KEYS + BLOCK) // CLEAR, clear, 0)
    value[KEYS:] = jnp.zeros((BLOCK, WIDTH), jnp.bfloat16)
    key[KEYS:] = jnp.zeros((BLOCK, WIDTH), jnp.bfloat16)
    dq_sum[...] = jnp.zeros_like(dq_sum)
    for i in range(PEERS):
        for h in range(HEADS):
            part = slice(h * WIDTH, (h + 1) * WIDTH)
            queries[i, h * ROWS : (h + 1) * ROWS] = q[i, :, part]
            grads[i, h * ROWS : (h + 1) * ROWS] = do[i, :, part]
    for copy in loads:
        copy.wait()

    def local_row(c, half):
        return pl.multiple_of(spans[2 * c + y_lo] * SPAN - base + half * ROWS, ROWS)

    def place_keys(i, _):
        for j in range(PEERS):
            for half in range(2):
                row = local_row(i * PEERS + j, half)
                key[pl.ds(row, ROWS)] = kv[half, i, 0, j * ROWS : (j + 1) * ROWS]
                value[pl.ds(row, ROWS)] = kv[half, i, 1, j * ROWS : (j + 1) * ROWS]
        return 0

    lax.fori_loop(0, RING, place_keys, 0)

    columns = HEADS * ROWS

    def plan(i, count):
        first = local_row(z * PEERS + i, core)
        row = first + lax.broadcasted_iota(jnp.int32, (1, columns), 1) % ROWS
        begin = jnp.int32(0)
        low = jnp.zeros((1, columns), jnp.int32)
        for n in range(starts.shape[0]):
            start = starts[n] - base
            begin = jnp.where(start <= first, jnp.maximum(begin, start), begin)
            low = jnp.where(start <= row, jnp.maximum(low, start), low)
        lows[i] = low
        highs[i] = row
        begin = (begin // ROWS) * ROWS
        steps = (first + ROWS - begin + BLOCK - 1) // BLOCK
        first_work[i] = count

        def enter(b, _):
            work_tile[count + b] = i
            work_row[count + b] = begin + b * BLOCK
            return 0

        lax.fori_loop(0, steps, enter, 0)
        return count + steps

    count = jnp.int32(0)
    for i in range(PEERS):
        count = plan(i, count)
    first_work[PEERS] = count
    for u in range(TOGETHER - 1):
        work_tile[count + u] = 0
        work_row[count + u] = KEYS
    groups = (count + TOGETHER - 1) // TOGETHER

    def score_group(g, _):
        products = []
        for u in range(TOGETHER):
            n = g * TOGETHER + u
            i = work_tile[n]
            here = pl.multiple_of(work_row[n], ROWS)
            rows = pl.ds(here, BLOCK)
            s = lax.dot_general(
                key[rows], queries[i], (((1,), (1,)), ((), ())), preferred_element_type=jnp.float32
            )
            dw = lax.dot_general(
                value[rows], grads[i], (((1,), (1,)), ((), ())), preferred_element_type=jnp.float32
            )
            products.append((here, lows[i], highs[i], s, dw))
        for u, (here, low, high, s, dw) in enumerate(products):
            n = g * TOGETHER + u
            pos = here + lax.broadcasted_iota(jnp.int32, (BLOCK, columns), 0)
            s = jnp.where((pos - low).astype(jnp.uint32) <= (high - low).astype(jnp.uint32), s * SCALE_LOG2, NEG_BIG)
            top = jnp.max(s, axis=0, keepdims=True)
            e = jnp.exp2(s - top)
            dweights[n] = dw
            powers[n] = s
            tops[pl.ds(n, 1)] = top
            totals[pl.ds(n, 1)] = jnp.sum(e, axis=0, keepdims=True)
            dots[pl.ds(n, 1)] = jnp.sum(e * dw, axis=0, keepdims=True)
        return 0

    lax.fori_loop(0, groups, score_group, 0)
    entry = lax.broadcasted_iota(jnp.int32, (WORK, 1), 0)
    for i in range(PEERS):
        mine = (entry >= first_work[i]) & (entry < first_work[i + 1])
        tops_i = jnp.where(mine, tops[:WORK], NEG_BIG)
        top = jnp.max(tops_i, axis=0, keepdims=True)
        factor = jnp.exp2(tops_i - top)
        total = jnp.sum(jnp.where(mine, totals[:WORK] * factor, 0.0), axis=0, keepdims=True)
        dot = jnp.sum(jnp.where(mine, dots[:WORK] * factor, 0.0), axis=0, keepdims=True)
        inverse = 1.0 / total
        tile_top[i] = top + jnp.log2(total)
        tile_inverse[i] = inverse
        tile_delta[i] = dot * inverse

    def grad_group(g, _):
        products = []
        for u in range(TOGETHER):
            n = g * TOGETHER + u
            i = work_tile[n]
            rows = pl.ds(pl.multiple_of(work_row[n], ROWS), BLOCK)
            w = jnp.exp2(powers[n] - tile_top[i])
            ds = (w * (dweights[n] - tile_delta[i])).astype(jnp.bfloat16)
            w = w.astype(jnp.bfloat16)
            products.append(
                (
                    i,
                    rows,
                    jnp.dot(w, grads[i], preferred_element_type=jnp.float32),
                    jnp.dot(ds, queries[i], preferred_element_type=jnp.float32),
                    lax.dot_general(
                        ds, key[rows], (((0,), (0,)), ((), ())), preferred_element_type=jnp.float32
                    ),
                )
            )
        for i, rows, to_value, to_key, to_query in products:
            dvalue[rows] += to_value
            dkey[rows] += to_key
            dq_sum[i] += to_query
        return 0

    lax.fori_loop(0, groups, grad_group, 0)
    for i in range(PEERS):
        out = (dq_sum[i] * SCALE).astype(jnp.bfloat16)
        for h in range(HEADS):
            dq[i, :, h * WIDTH : (h + 1) * WIDTH] = out[h * ROWS : (h + 1) * ROWS]

    def give_keys(i, _):
        for j in range(PEERS):
            for half in range(2):
                rows = pl.ds(local_row(i * PEERS + j, half), ROWS)
                slot = slice(j * ROWS, (j + 1) * ROWS)
                dkv[half, i, 0, slot] = (dkey[rows] * SCALE).astype(jnp.bfloat16)
                dkv[half, i, 1, slot] = dvalue[rows].astype(jnp.bfloat16)
        return 0

    lax.fori_loop(0, RING, give_keys, 0)


def scatter_kernel(
    dqp, dkv, dq, dk, dv, pair, got, sent, final,
    pair_s, pair_r, q_s, q_r, ring_s, ring_r, kv_s, kv_r, row,
):
    z, p, t, y_lo, core = place()
    here = z * PEERS + p
    sibling = y_lo * 2 + 1 - core
    across, large, ring, small = {}, [], {}, []
    greet(z, p, t, sibling, row)
    def exchange(offsets):
        for offset in offsets:
            across[offset] = remote(
                dkv.at[1 - core, (z + offset) % RING],
                pair.at[offset],
                pair_s.at[offset],
                pair_r.at[offset],
                (here, sibling),
            )

    exchange((4, 3, 5))
    met = set()

    def term(offset, part, half):
        if offset not in met:
            across[offset].wait_recv()
            met.add(offset)
        rows = half_rows(p, half)
        mine = dkv[core, (z + offset) % RING, part, rows].astype(jnp.float32)
        return mine + pair[offset, part, rows].astype(jnp.float32)

    def arrived(step, way, part, half):
        ring[step, way, part, half].wait_recv()
        return got[step, way, part, half_rows(p, half)].astype(jnp.float32)

    def send(step, way, part, half, value):
        rows = half_rows(p, half)
        key = step, way, part, half
        sent[step, way, part, rows] = value.astype(jnp.bfloat16)
        ring[key] = remote(
            sent.at[step, way, part, rows],
            got.at[step, way, part, rows],
            ring_s.at[key],
            ring_r.at[key],
            beside(z, p, t, way, 2 if step == 3 else 1),
        )

    for step in range(3):
        for half in (1, 0):
            if step == 0:
                for way in range(2):
                    send(3, way, way, half, term(4, way, half))
            for part in range(2):
                for way in range(2):
                    value = term(3 - step if way == 0 else RING - 3 + step, part, half)
                    if step > 0:
                        value += arrived(step - 1, way, part, half)
                    if step == 1 and part == way:
                        value += arrived(3, way, part, half)
                    send(step, way, part, half, value)
        if step == 0:
            exchange((2, 6, 1, 7, 0))
            pl.semaphore_wait(row, 1)
            wide = HEADS * WIDTH
            columns = pl.ds(pl.multiple_of(p * wide, wide), wide)
            for d in ORDER:
                other = peer_of(p, d)
                large.append(
                    remote(
                        dqp.at[other], dq.at[:, columns], q_s.at[d], q_r.at[d], (z * PEERS + other, t)
                    )
                )
            own_large = pltpu.make_async_copy(dqp.at[p], dq.at[:, columns], q_s.at[0])
            own_large.start()
    narrow = pl.ds(pl.multiple_of(p * WIDTH, WIDTH), WIDTH)
    own_small = []
    for half in (1, 0):
        for part, dst in enumerate((dk, dv)):
            value = term(0, part, half)
            for way in range(2):
                value += arrived(2, way, part, half)
            final[part, half_rows(p, half)] = value.astype(jnp.bfloat16)
            for d in range(PEERS):
                if d // 4 != half:
                    continue
                other = peer_of(p, d)
                src = final.at[part, pl.ds(other * ROWS, ROWS)]
                if d == 0:
                    copy = pltpu.make_async_copy(src, dst.at[:, narrow], kv_s.at[0, part])
                    copy.start()
                    own_small.append(copy)
                else:
                    small.append(
                        remote(
                            src,
                            dst.at[:, narrow],
                            kv_s.at[d, part],
                            kv_r.at[d, part],
                            (z * PEERS + other, t),
                        )
                    )
    for copy in large + small:
        copy.wait()
    for copy in [own_large] + own_small:
        copy.wait()
    for copy in list(ring.values()) + list(across.values()):
        copy.wait_send()


def attend(span_map, doc_starts, qg, dog, kv):
    vmem = pl.BlockSpec(memory_space=pltpu.VMEM)
    hbm = pl.BlockSpec(memory_space=pltpu.HBM)
    dma = pltpu.SemaphoreType.DMA
    b16, f32 = jnp.bfloat16, jnp.float32
    columns = HEADS * ROWS
    return pl.pallas_call(
        attention_kernel,
        out_shape=(
            jax.ShapeDtypeStruct(qg.shape, b16),
            jax.ShapeDtypeStruct(kv.shape, b16),
        ),
        in_specs=[hbm, hbm, vmem, vmem, vmem],
        out_specs=(vmem, vmem),
        scratch_shapes=[
            pltpu.SMEM(span_map.shape, jnp.int32),
            pltpu.SMEM(doc_starts.shape, jnp.int32),
            pltpu.SMEM((WORK + TOGETHER,), jnp.int32),
            pltpu.SMEM((WORK + TOGETHER,), jnp.int32),
            pltpu.SMEM((PEERS + 1,), jnp.int32),
            pltpu.VMEM((KEYS + BLOCK, WIDTH), b16),
            pltpu.VMEM((KEYS + BLOCK, WIDTH), b16),
            pltpu.VMEM((KEYS + BLOCK, WIDTH), f32),
            pltpu.VMEM((KEYS + BLOCK, WIDTH), f32),
            pltpu.VMEM((PEERS, columns, WIDTH), b16),
            pltpu.VMEM((PEERS, columns, WIDTH), b16),
            pltpu.VMEM((PEERS, 1, columns), jnp.int32),
            pltpu.VMEM((PEERS, 1, columns), jnp.int32),
            pltpu.VMEM((WORK + TOGETHER, BLOCK, columns), f32),
            pltpu.VMEM((WORK + TOGETHER, BLOCK, columns), f32),
            pltpu.VMEM((WORK + 8 + TOGETHER, columns), f32),
            pltpu.VMEM((WORK + 8 + TOGETHER, columns), f32),
            pltpu.VMEM((WORK + 8 + TOGETHER, columns), f32),
            pltpu.VMEM((PEERS, 1, columns), f32),
            pltpu.VMEM((PEERS, 1, columns), f32),
            pltpu.VMEM((PEERS, 1, columns), f32),
            pltpu.VMEM((PEERS, columns, WIDTH), f32),
            dma((2,)),
        ],
        compiler_params=pltpu.CompilerParams(vmem_limit_bytes=48 * 1024 * 1024),
        name="attention_grads",
    )(span_map, doc_starts, qg, dog, kv)


def gather(queries, output_gradient, key_head_states, value_head_states):
    anywhere = pl.BlockSpec(memory_space=pl.ANY)
    vmem = pl.BlockSpec(memory_space=pltpu.VMEM)
    hbm = pl.BlockSpec(memory_space=pltpu.HBM)
    dma = pltpu.SemaphoreType.DMA
    b16 = jnp.bfloat16
    wide = HEADS * WIDTH
    rows = PEERS * ROWS
    grouped = jax.ShapeDtypeStruct((PEERS, ROWS, wide), b16)
    chunks = jax.ShapeDtypeStruct((2, RING, 2, rows, WIDTH), b16)
    return pl.pallas_call(
        gather_kernel,
        out_shape=(grouped, grouped, chunks),
        in_specs=[hbm] * 4,
        out_specs=(anywhere,) * 3,
        scratch_shapes=[
            dma((PEERS, 2)),
            dma((PEERS, 2)),
            dma((PEERS, 2)),
            dma((PEERS, 2)),
            dma((4, 2, 2, 2)),
            dma((4, 2, 2, 2)),
            dma((RING, 2, 2)),
            dma((RING, 2, 2)),
            pltpu.SemaphoreType.REGULAR,
        ],
        compiler_params=pltpu.CompilerParams(
            collective_id=0, has_side_effects=True, vmem_limit_bytes=2 * 1024 * 1024
        ),
        name="gather_heads",
    )(queries, output_gradient, key_head_states, value_head_states)


def scatter(dqp, dkv):
    anywhere = pl.BlockSpec(memory_space=pl.ANY)
    vmem = pl.BlockSpec(memory_space=pltpu.VMEM)
    hbm = pl.BlockSpec(memory_space=pltpu.HBM)
    dma = pltpu.SemaphoreType.DMA
    b16 = jnp.bfloat16
    wide = HEADS * WIDTH
    rows = PEERS * ROWS
    return pl.pallas_call(
        scatter_kernel,
        out_shape=(
            jax.ShapeDtypeStruct((ROWS, PEERS * wide), b16),
            jax.ShapeDtypeStruct((ROWS, PEERS * WIDTH), b16),
            jax.ShapeDtypeStruct((ROWS, PEERS * WIDTH), b16),
        ),
        in_specs=[anywhere, vmem],
        out_specs=(anywhere,) * 3,
        scratch_shapes=[
            pltpu.VMEM((RING, 2, rows, WIDTH), b16),
            pltpu.VMEM((4, 2, 2, rows, WIDTH), b16),
            pltpu.VMEM((4, 2, 2, rows, WIDTH), b16),
            pltpu.VMEM((2, rows, WIDTH), b16),
            dma((RING,)),
            dma((RING,)),
            dma((PEERS,)),
            dma((PEERS,)),
            dma((4, 2, 2, 2)),
            dma((4, 2, 2, 2)),
            dma((PEERS, 2)),
            dma((PEERS, 2)),
            pltpu.SemaphoreType.REGULAR,
        ],
        compiler_params=pltpu.CompilerParams(
            collective_id=1, has_side_effects=True, vmem_limit_bytes=12 * 1024 * 1024
        ),
        name="scatter_grads",
    )(dqp, dkv)


def finish_kernel(dq_in, dk_in, dv_in, dq, dk, dv, sems):
    copies = [
        pltpu.make_async_copy(src, dst, sems.at[n])
        for n, (src, dst) in enumerate(((dq_in, dq), (dk_in, dk), (dv_in, dv)))
    ]
    for copy in copies:
        copy.start()
    for copy in copies:
        copy.wait()


def finish(*grads):
    anywhere = pl.BlockSpec(memory_space=pl.ANY)
    hbm = pl.BlockSpec(memory_space=pltpu.HBM)
    return pl.pallas_call(
        finish_kernel,
        out_shape=tuple(jax.ShapeDtypeStruct(x.shape, x.dtype) for x in grads),
        in_specs=[anywhere] * 3,
        out_specs=(hbm,) * 3,
        scratch_shapes=[pltpu.SemaphoreType.DMA((3,))],
        compiler_params=pltpu.CompilerParams(vmem_limit_bytes=1024 * 1024),
        name="finish",
    )(*grads)


def shards(queries, key_head_states, value_head_states, output_gradient, doc_starts, span_map):
    queries, output_gradient, key_head_states, value_head_states, span_map, doc_starts = (
        pltpu.with_memory_space_constraint(x, pltpu.HBM)
        for x in (queries, output_gradient, key_head_states, value_head_states, span_map, doc_starts)
    )
    qg, dog, kv = gather(queries, output_gradient, key_head_states, value_head_states)
    dqp, dkv = attend(span_map, doc_starts, qg, dog, kv)
    return finish(*scatter(dqp, dkv))


def solution(mesh):
    rows = P(("ctx", "tp"), None)
    in_specs = (rows, rows, rows, rows, P(), P())
    return jax.shard_map(
        shards, mesh=mesh, in_specs=in_specs, out_specs=(rows, rows, rows), check_vma=False
    )
```
